32 devices in a mesh: tm: 8 (over z, core), row: 4 (over y, x).
Axes of the slice: x: 2, y: 2, z: 4, core: 2. Of those that a mesh axis runs over, the one named last changes fastest.
Arguments:
- covariance: float32 [8, 1024, 1024], P('tm', 'row'), as said below
- precision: float32 [8, 1024, 1024], P('tm', 'row'), as said below
- band_weight: float32 [8, 5, 1024], P('tm'), may hold values from -0.5 to 0.5
- band_offset: int32 [8, 5], P('tm'), may hold values from -64 to 64, as said below
- prior_mean: float32 [8, 1024], P('tm', 'row'), may hold values from -6 to 6
- innovation: float32 [8, 128], P('tm'), may hold values from -6 to 6
- seen_sites: int32 [8, 128], P('tm'), may hold values from 0 to 511, as said below
Outputs:
- smoother_gain: float32 [8, 1024, 1024], P('tm', 'row')
- smoother_shift: float32 [8, 1024], P('tm', 'row')
- smoother_spread: float32 [8, 1024, 1024], P('tm', 'row')
The draws below stay inside these ranges and needn't reach their ends.
Inputs may be any that keep to these rules, and one draw needn't show every extreme that they name: `covariance`: each block's matrix is symmetric. `precision`: each block's matrix is symmetric. `band_offset`: the offsets of one block are distinct, and one of them has magnitude 64. `seen_sites`: the sites of one step are distinct.
All inputs are finite; a program needn't handle non-finite values.
Results may differ from the reference program's by a relative error of at most 0.0003.
Values sent between devices are 32-bit elements; how exact they have to be, the bound alone decides.
A program may use at most 64 MiB of HBM per device.

```python
import math
import jax
import jax.numpy as jnp
from jax import lax

SITES = 512
STATE = 1024
NBAND = 5
REACH = 64
OBS = 128
TBLOCKS = 8


def symmetric_draw(key, lowest, highest, mixing):
    first_key, second_key = jax.random.split(key, 2)
    raw_entries = jax.random.uniform(first_key, (TBLOCKS, STATE, STATE), jnp.float32, -1.0, 1.0)
    mixed = (raw_entries + jnp.swapaxes(raw_entries, 1, 2)) * (mixing / math.sqrt(STATE))
    diagonal = jax.random.uniform(second_key, (TBLOCKS, STATE), jnp.float32, lowest, highest)
    matrix = mixed + diagonal[:, :, None] * jnp.eye(STATE, dtype=jnp.float32)[None, :, :]
    return matrix


def draw_covariance(key, part):
    key = jax.random.fold_in(key, 11)
    return symmetric_draw(key, 0.5, 1.0, 0.25)


def draw_precision(key, part):
    key = jax.random.fold_in(key, 12)
    return symmetric_draw(key, 0.5, 1.0, 0.25)


def shuffle_row(row_key, values):
    return jax.random.permutation(row_key, values)


def draw_band_offset(key, part):
    key = jax.random.fold_in(key, 13)
    sign_key, pick_key, order_key = jax.random.split(key, 3)
    signs = jax.random.randint(sign_key, (TBLOCKS,), 0, 2).astype(jnp.int32)
    choices_pool = jnp.arange(2 * REACH, dtype=jnp.int32)[None, :] - REACH + signs[:, None]
    picked = jax.vmap(shuffle_row)(jax.random.split(pick_key, TBLOCKS), choices_pool)[:, :NBAND - 1]
    extreme = REACH * (1 - 2 * signs)
    joined = jnp.concatenate([extreme[:, None], picked], axis=1)
    orders = jax.vmap(shuffle_row)(jax.random.split(order_key, TBLOCKS), jnp.broadcast_to(jnp.arange(NBAND, dtype=jnp.int32), (TBLOCKS, NBAND)))
    return jnp.take_along_axis(joined, orders, axis=1).astype(jnp.int32)


def draw_seen_sites(key, part):
    key = jax.random.fold_in(key, 14)
    every_site = jnp.broadcast_to(jnp.arange(SITES, dtype=jnp.int32), (TBLOCKS, SITES))
    shuffled = jax.vmap(shuffle_row)(jax.random.split(key, TBLOCKS), every_site)
    return shuffled[:, :OBS].astype(jnp.int32)


def block_scale(stream_key, dims, pieces, low, high):
    level, own = 1.0, jax.random.fold_in(stream_key, 6)
    for position, parts in pieces:
        heights = jnp.exp(jax.random.uniform(jax.random.fold_in(own, position), (parts,), jnp.float32, low / len(pieces), high / len(pieces)))
        level = level * jnp.repeat(heights, dims[position] // parts).reshape([-1 if axis == position else 1 for axis in range(len(dims))])
    return level


def centred(key, shape, scale, bound, cuts=(), kind=jnp.bfloat16):
    loudness = block_scale(key, shape, cuts, -0.22, 0.18) if cuts else 1.0
    values = jax.random.normal(key, shape, jnp.float32) * scale * loudness
    return jnp.minimum(jnp.maximum(values, -bound), bound).astype(kind)


def setup_inputs(seed: int = 0) -> dict:
    key_list = jax.random.split(jax.random.key(seed), 8)
    return {
        "covariance": draw_covariance(jax.random.fold_in(key_list[7], 71), 0),
        "precision": draw_precision(jax.random.fold_in(key_list[7], 71), 0),
        "band_weight": jnp.clip(jax.random.uniform(key_list[2], (TBLOCKS, NBAND, STATE), jnp.float32, -0.5, 0.5) * block_scale(key_list[2], (TBLOCKS, NBAND, STATE), ((0, 8),), -0.4, 0.0), -0.5, 0.5),
        "band_offset": draw_band_offset(jax.random.fold_in(key_list[7], 71), 0),
        "prior_mean": centred(key_list[4], (TBLOCKS, STATE), 1.0, 6.0, ((0, 8), (1, 4)), jnp.float32),
        "innovation": centred(key_list[5], (TBLOCKS, OBS), 1.0, 6.0, ((0, 8),), jnp.float32),
        "seen_sites": draw_seen_sites(jax.random.fold_in(key_list[7], 71), 0),
    }


HIGHEST = lax.Precision.HIGHEST


def product(left, right):
    return jnp.dot(left, right, precision=HIGHEST, preferred_element_type=jnp.float32)


def against(left, right):
    return lax.dot_general(left, right, (((1,), (1,)), ((), ())), precision=HIGHEST, preferred_element_type=jnp.float32)


def band_columns(matrix, weights, offsets):
    columns = matrix.shape[1]
    padded = jnp.pad(matrix, ((0, 0), (REACH, REACH)))
    summed = jnp.zeros(matrix.shape, jnp.float32)
    for band_index in range(NBAND):
        start_at = (offsets[band_index] + REACH).astype(jnp.int32)
        sliced = lax.dynamic_slice_in_dim(padded, start_at, columns, 1)
        summed = summed + weights[band_index][None, :] * sliced
    return summed


def band_vector(vector, weights, offsets):
    padded = jnp.pad(vector, (REACH, REACH))
    summed = jnp.zeros(vector.shape, jnp.float32)
    for band_index in range(NBAND):
        start_at = (offsets[band_index] + REACH).astype(jnp.int32)
        summed = summed + weights[band_index] * lax.dynamic_slice_in_dim(padded, start_at, STATE, 0)
    return summed


def element(inputs):
    matrix, inverse, weights, offsets, mean_block, innov_block, site_block = inputs
    crossed = band_columns(matrix, weights, offsets)
    gain = product(crossed, inverse)
    spread = matrix - against(crossed, gain)
    matches = (site_block[:, None] == jnp.arange(STATE, dtype=jnp.int32)[None, :]).astype(jnp.float32)
    pulled = product(innov_block, matches)
    filtered = mean_block + product(matrix, pulled)
    forward = band_vector(filtered, weights, offsets)
    shift = filtered - product(gain, forward)
    return gain, shift, spread


def combine(first_gain, first_shift, first_spread, later_gain, later_shift, later_spread):
    merged_gain = product(first_gain, later_gain)
    merged_shift = product(first_gain, later_shift) + first_shift
    merged_spread = against(product(first_gain, later_spread), first_gain) + first_spread
    return merged_gain, merged_shift, merged_spread


def reference(covariance, precision, band_weight, band_offset, prior_mean, innovation, seen_sites):
    gains, shifts, spreads = lax.map(element, (covariance, precision, band_weight, band_offset, prior_mean, innovation, seen_sites))
    for stride in (1, 2):
        def level(block):
            later = jnp.minimum(block + stride, TBLOCKS - 1)
            merged = combine(gains[block], shifts[block], spreads[block], gains[later], shifts[later], spreads[later])
            inside = block + stride < TBLOCKS
            return (jnp.where(inside, merged[0], gains[block]),
                    jnp.where(inside, merged[1], shifts[block]),
                    jnp.where(inside, merged[2], spreads[block]))
        gains, shifts, spreads = lax.map(level, jnp.arange(TBLOCKS, dtype=jnp.int32))
    return gains, shifts, spreads
```

```python
import jax
import jax.numpy as jnp
from jax import lax
from jax.sharding import PartitionSpec as P

NBAND = 5
REACH = 64
SPAN = 3

HIGH = lax.Precision.HIGH
HIGHEST = lax.Precision.HIGHEST


def dot(left, right):
    return jnp.dot(left, right, precision=HIGH, preferred_element_type=jnp.float32)


def band(matrix, weights, offsets):
    columns = matrix.shape[1]
    padded = jnp.pad(matrix, ((0, 0), (REACH, REACH)))
    summed = jnp.zeros(matrix.shape, jnp.float32)
    for b in range(NBAND):
        sliced = lax.dynamic_slice_in_dim(padded, offsets[b] + REACH, columns, 1)
        summed = summed + weights[b][None, :] * sliced
    return summed


def band_back(matrix, weights, offsets):
    columns = matrix.shape[1]
    padded = jnp.pad(matrix, ((0, 0), (REACH, REACH)))
    padded_weights = jnp.pad(weights, ((0, 0), (REACH, REACH)))
    summed = jnp.zeros(matrix.shape, jnp.float32)
    for b in range(NBAND):
        start = REACH - offsets[b]
        sliced = lax.dynamic_slice_in_dim(padded, start, columns, 1)
        scale = lax.dynamic_slice_in_dim(padded_weights[b], start, columns, 0)
        summed = summed + scale[None, :] * sliced
    return summed


def body(covariance, precision, band_weight, band_offset, prior_mean, innovation, seen_sites):
    cov_rows = covariance[0]
    weights = band_weight[0]
    offsets = band_offset[0]
    columns = cov_rows.shape[1]
    count = lax.axis_size("tm")
    up_route = [(i, i + 1) for i in range(count - 1)]
    down_route = [(i + 1, i) for i in range(count - 1)]

    inverse = lax.all_gather(precision[0], "row", axis=0, tiled=True)
    cov = lax.all_gather(cov_rows, "row", axis=0, tiled=True)
    matches = (seen_sites[0][:, None] == jnp.arange(columns, dtype=jnp.int32)[None, :]).astype(
        jnp.float32
    )
    pulled = jnp.dot(innovation[0], matches, precision=HIGHEST)
    filtered_rows = prior_mean[0] + jnp.sum(cov_rows * pulled[None, :], axis=1)
    filtered = lax.all_gather(filtered_rows, "row", axis=0, tiled=True)
    forward = band(filtered[None, :], weights, offsets)

    gain = dot(band(cov_rows, weights, offsets), inverse)
    gains, works = [gain], [cov_rows]
    parts = [filtered_rows - jnp.sum(gain * forward, axis=1)]
    time_index = lax.axis_index("tm")
    final = gain
    for s in range(1, SPAN + 1):
        arrived = lax.ppermute(gain, "tm", up_route)
        work = dot(arrived, cov)
        gain = dot(band(work, weights, offsets), inverse)
        gains.append(gain)
        works.append(work)
        parts.append(
            jnp.sum(arrived * filtered[None, :], axis=1) - jnp.sum(gain * forward, axis=1)
        )
        if s < SPAN:
            home = [(count - 1, count - 1 - s)]
            back = lax.ppermute(gain, "tm", home)
            final = jnp.where(time_index == count - 1 - s, back, final)
        else:
            home = [(i + s, i) for i in range(count - s)]
            back = lax.ppermute(gain, "tm", home)
            final = jnp.where(time_index < count - s, back, final)
    spread = works[SPAN] - dot(band_back(gains[SPAN], weights, offsets), cov)
    shift = parts[SPAN]
    for s in range(SPAN - 1, -1, -1):
        later = lax.ppermute(spread, "tm", down_route)
        shift = lax.ppermute(shift, "tm", down_route) + parts[s]
        inner = dot(later, inverse) - gains[s]
        spread = works[s] + dot(band_back(inner, weights, offsets), cov)
    return (final[None], shift[None], spread[None])


def solution(mesh):
    in_specs = (
        P("tm", "row", None),
        P("tm", "row", None),
        P("tm", None, None),
        P("tm", None),
        P("tm", "row"),
        P("tm", None),
        P("tm", None),
    )
    out_specs = (P("tm", "row", None), P("tm", "row"), P("tm", "row", None))
    return jax.shard_map(body, mesh=mesh, in_specs=in_specs, out_specs=out_specs, check_vma=False)
```

```python
import functools

import jax
import jax.numpy as jnp
from jax import lax
from jax.experimental import pallas as pl
from jax.experimental.pallas import tpu as pltpu
from jax.sharding import PartitionSpec as P

NBAND = 5
REACH = 64
SPAN = 3
TILE = 256
EDGE = 128
VEC = 16

MESH = pl.DeviceIdType.MESH
F32 = jnp.float32
BF16 = jnp.bfloat16


def split(value):
    high = value.astype(BF16)
    return high, (value - high.astype(F32)).astype(BF16)


def dot3(left, right):
    (lh, ll), (rh, rl) = left, right
    one = functools.partial(jnp.dot, preferred_element_type=F32)
    return one(lh, rh) + (one(lh, rl) + one(ll, rh))


def dot3t(left, right):
    (lh, ll), (rh, rl) = left, right

    def one(a, b):
        return lax.dot_general(a, b, (((1,), (1,)), ((), ())), preferred_element_type=F32)

    return one(lh, rh) + (one(lh, rl) + one(ll, rh))


def kernel(
    n, n_row,
    offsets, cov_rows, inv_rows, weights, prior, innovation, seen,
    gain_out, shift_out, spread_out,
    cov_land, inv_land, cov_h, cov_l, inv_h, inv_l, ft_h, ft_l,
    x_in, x_keep, w_keep, v_in, v_out, a_h, a_l, pad_h, pad_l, acc, pad_acc,
    prior_all, f_h, f_l, h_h, h_l, part, vec_in, vec_out,
    g_send, g_recv, p_send, p_recv, x_send, x_recv, home_send, home_recv,
    v_send, v_recv, vec_send, vec_recv,
):
    tm = lax.axis_index("tm")
    row = lax.axis_index("row")
    rows, columns = cov_rows.shape
    tiles = columns // TILE

    def at(index, size):
        return pl.ds(pl.multiple_of(index * size, size), size)

    barrier = pltpu.get_barrier_semaphore()

    def greet(t, r):
        pl.semaphore_signal(barrier, inc=1, device_id=(t, r), device_id_type=MESH)

    for d in range(1, n_row):
        greet(tm, lax.rem(row + d, n_row))
    for d in range(1, SPAN + 1):
        pl.when(tm + d < n)(lambda d=d: greet(tm + d, row))
        pl.when(tm - d >= 0)(lambda d=d: greet(tm - d, row))
    pl.semaphore_wait(
        barrier, n_row - 1 + jnp.minimum(tm, SPAN) + jnp.minimum(n - 1 - tm, SPAN)
    )

    square = n_row == 4
    if square:
        x, y = lax.rem(row, 2), row // 2
        r1, r2, r3 = 2 * y + 1 - x, 2 * (1 - y) + x, 2 * (1 - y) + 1 - x
    half = rows // 2

    def pieces(m, src, land):
        def copy(c, to, rsl, csl, drow):
            return pltpu.make_async_remote_copy(
                src_ref=src.at[rsl, csl], dst_ref=land.at[drow, csl],
                send_sem=g_send.at[m, c], recv_sem=g_recv.at[m, c],
                device_id=(tm, to), device_id_type=MESH,
            )

        every = pl.ds(0, rows)
        if not square:
            return [
                copy(d - 1, lax.rem(row + d, n_row), every, pl.ds(0, columns), at(row, rows))
                for d in range(1, n_row)
            ]
        right = pl.ds(pl.multiple_of(r3 * rows + half, half), half)
        upper = pl.ds(pl.multiple_of(row * rows, rows), half)
        mine = at(row, rows)
        return [
            copy(0, r1, every, at(row, rows), mine),
            copy(1, r2, every, at(row, rows), mine),
            copy(2, r3, every, at(row, rows), mine),
            copy(3, r1, every, at(r2, rows), mine),
            copy(4, r2, every, at(r1, rows), mine),
            copy(5, r1, pl.ds(0, half), at(r3, rows), upper),
            copy(6, r2, every, right, mine),
        ]

    def fill(src, land, high, low):
        def put(rsl, csl, value):
            h, l = split(value)
            high[rsl, csl] = h
            low[rsl, csl] = l

        if not square:
            land[at(row, rows), :] = src[...]

            def every(r, carry):
                rsl = at(r, TILE)
                put(rsl, pl.ds(0, columns), land[rsl, :])
                return carry

            lax.fori_loop(0, columns // TILE, every, 0)
            return
        put(at(row, rows), pl.ds(0, columns), src[...])
        for r in (r1, r2, r3):
            put(at(r, rows), at(row, rows), src[:, at(r, rows)].T)
            put(at(r, rows), at(r, rows), land[at(r, rows), at(r, rows)])
        for r in (r1, r2):
            block = land[at(r, rows), at(r3, rows)]
            put(at(r, rows), at(r3, rows), block)
            put(at(r3, rows), at(r, rows), block.T)
        upper = pl.ds(pl.multiple_of(r1 * rows, rows), half)
        lower = pl.ds(pl.multiple_of(r1 * rows + half, half), half)
        block = land[upper, at(r2, rows)]
        put(upper, at(r2, rows), block)
        put(at(r2, rows), upper, block.T)
        block = land[at(r2, rows), lower]
        put(at(r2, rows), lower, block)
        put(lower, at(r2, rows), block.T)

    inv_copies = pieces(0, inv_rows, inv_land)
    cov_copies = pieces(1, cov_rows, cov_land)
    for c in inv_copies:
        c.start()

    prior_all[row] = prior[...]
    prior_copies = [
        pltpu.make_async_remote_copy(
            src_ref=prior, dst_ref=prior_all.at[row],
            send_sem=p_send.at[d - 1], recv_sem=p_recv.at[d - 1],
            device_id=(tm, lax.rem(row + d, n_row)), device_id_type=MESH,
        )
        for d in range(1, n_row)
    ]
    for c in prior_copies:
        c.start()

    window = TILE + 2 * EDGE
    apart = lax.broadcasted_iota(jnp.int32, (window, TILE), 0) - (
        lax.broadcasted_iota(jnp.int32, (window, TILE), 1) + EDGE
    )
    for t in range(tiles):
        total = jnp.zeros((window, TILE), F32)
        for b in range(NBAND):
            scale = weights[b : b + 1, t * TILE : (t + 1) * TILE]
            total = total + jnp.where(apart == offsets[0, b], scale, 0.0)
        h, l = split(total)
        ft_h[t] = h
        ft_l[t] = l

    zeros = jnp.zeros((rows, EDGE), BF16)
    for ref in (pad_h, pad_l):
        ref[:, :EDGE] = zeros
        ref[:, EDGE + columns :] = zeros

    def full(t):
        return pl.ds(pl.multiple_of(t * TILE, TILE), TILE)

    def x_copy(s, t):
        return pltpu.make_async_remote_copy(
            src_ref=x_keep.at[s, :, full(t)], dst_ref=x_in.at[s, :, full(t)],
            send_sem=x_send.at[s, t], recv_sem=x_recv.at[s, t],
            device_id=(tm + 1, row), device_id_type=MESH,
        )

    def home_copy(s, t):
        return pltpu.make_async_remote_copy(
            src_ref=x_keep.at[s, :, full(t)], dst_ref=gain_out.at[:, full(t)],
            send_sem=home_send.at[s, t], recv_sem=home_recv.at[t],
            device_id=(tm - s, row), device_id_type=MESH,
        )

    def v_copy(s, t):
        return pltpu.make_async_remote_copy(
            src_ref=v_out.at[s, :, full(t)], dst_ref=v_in.at[s, :, full(t)],
            send_sem=v_send.at[s, t], recv_sem=v_recv.at[s, t],
            device_id=(tm - 1, row), device_id_type=MESH,
        )

    def vec_copy(s):
        return pltpu.make_async_remote_copy(
            src_ref=vec_out.at[s], dst_ref=vec_in.at[s],
            send_sem=vec_send.at[s], recv_sem=vec_recv.at[s],
            device_id=(tm - 1, row), device_id_type=MESH,
        )

    def goes_up(s):
        return (tm >= s) & (s < SPAN) & (tm + 1 < n)

    def goes_home(s):
        return (tm >= s) & (s > 0) & ((s == SPAN) | (tm == n - 1))

    def goes_down(s):
        return (tm >= s) & (s > 0)

    def band_step(s):
        h, l = split(w_keep[s])
        pad_h[:, EDGE : EDGE + columns] = h
        pad_l[:, EDGE : EDGE + columns] = l
        for t in range(tiles):
            wide = slice(t * TILE, t * TILE + window)
            h, l = split(dot3((pad_h[:, wide], pad_l[:, wide]), (ft_h[t], ft_l[t])))
            a_h[:, t * TILE : (t + 1) * TILE] = h
            a_l[:, t * TILE : (t + 1) * TILE] = l

    def gain_step(s):
        def one(t, carry):
            x_keep[s, :, full(t)] = dot3(
                (a_h[...], a_l[...]), (inv_h[:, full(t)], inv_l[:, full(t)])
            )
            pl.when(goes_up(s))(lambda: x_copy(s, t).start())
            pl.when(goes_home(s))(lambda: home_copy(s, t).start())
            return carry

        lax.fori_loop(0, tiles, one, 0)

    def against_vec(high, low, block):
        return dot3t((high[...], low[...]), split(block))

    w_keep[0] = cov_rows[...]
    band_step(0)
    for c in inv_copies:
        c.wait_send()
    for c in cov_copies:
        c.start()
    for c in inv_copies:
        c.wait_recv()
    fill(inv_rows, inv_land, inv_h, inv_l)
    gain_step(0)

    sites = lax.broadcasted_iota(jnp.int32, (seen.shape[0], columns), 1)
    matches = jnp.where(sites == seen[...], 1.0, 0.0).astype(BF16)
    first, second = split(innovation[...])
    third = (innovation[...] - first.astype(F32) - second.astype(F32)).astype(BF16)
    pulled = jnp.zeros((VEC, columns), F32)
    for piece in (third, second, first):
        pulled = pulled + jnp.dot(piece, matches, preferred_element_type=F32)
    pulled = split(pulled)
    own = prior[...] + dot3t(pulled, split(cov_rows[...]))
    for c in prior_copies:
        c.wait()
    for c in cov_copies:
        c.wait()
    fill(cov_rows, cov_land, cov_h, cov_l)
    prior_row = jnp.concatenate([prior_all[r] for r in range(n_row)], axis=1)
    for t in range(tiles):
        cols = slice(t * TILE, (t + 1) * TILE)
        value = prior_row[:, cols] + dot3(pulled, (cov_h[:, cols], cov_l[:, cols]))
        h, l = split(value)
        f_h[:, EDGE + t * TILE : EDGE + (t + 1) * TILE] = h
        f_l[:, EDGE + t * TILE : EDGE + (t + 1) * TILE] = l
    zeros = jnp.zeros((VEC, EDGE), BF16)
    for ref in (f_h, f_l):
        ref[:, :EDGE] = zeros
        ref[:, EDGE + columns :] = zeros
    for t in range(tiles):
        wide = slice(t * TILE, t * TILE + window)
        h, l = split(dot3((f_h[:, wide], f_l[:, wide]), (ft_h[t], ft_l[t])))
        h_h[:, t * TILE : (t + 1) * TILE] = h
        h_l[:, t * TILE : (t + 1) * TILE] = l
    part[0] = own - against_vec(h_h, h_l, x_keep[0])

    @pl.when(tm == n - 1)
    def _():
        gain_out[...] = x_keep[0]

    inside = slice(EDGE, EDGE + columns)

    def forward(s, carry):
        @pl.when(tm >= s)
        def _():
            w_keep[s] = jnp.zeros((rows, columns), F32)

            def one(t, carry):
                x_copy(s - 1, t).wait_recv()
                piece = split(x_in[s - 1, :, full(t)])
                for c in range(0, columns, 2 * TILE):
                    cols = slice(c, c + 2 * TILE)
                    w_keep[s, :, cols] += dot3(
                        piece, (cov_h[full(t), cols], cov_l[full(t), cols])
                    )
                return carry

            lax.fori_loop(0, tiles, one, 0)
            band_step(s)
            gain_step(s)
            part[s] = dot3t(
                (f_h[:, inside], f_l[:, inside]), split(x_in[s - 1])
            ) - against_vec(h_h, h_l, x_keep[s])

        return carry

    lax.fori_loop(1, SPAN + 1, forward, 0)

    def backward(i, carry):
        s = SPAN - i

        @pl.when(tm >= s)
        def _():
            acc[...] = -x_keep[s]
            vec_out[s] = part[s]

            @pl.when((s < SPAN) & (tm < n - 1))
            def _():
                def one(t, carry):
                    v_copy(s + 1, t).wait_recv()
                    piece = split(v_in[s + 1, :, full(t)])
                    for c in range(0, columns, 2 * TILE):
                        cols = slice(c, c + 2 * TILE)
                        acc[:, cols] += dot3(
                            piece, (inv_h[full(t), cols], inv_l[full(t), cols])
                        )
                    return carry

                lax.fori_loop(0, tiles, one, 0)
                vec_copy(s + 1).wait_recv()
                vec_out[s] += vec_in[s + 1]

            pl.when(goes_down(s))(lambda: vec_copy(s).start())
            pad_acc[...] = jnp.zeros(pad_acc.shape, F32)
            for t in range(tiles):
                wide = slice(t * TILE, t * TILE + window)
                piece = split(acc[:, t * TILE : (t + 1) * TILE])
                pad_acc[:, wide] += dot3t(piece, (ft_h[t], ft_l[t]))
            h, l = split(pad_acc[:, inside])
            a_h[...] = h
            a_l[...] = l

            def last(t, carry):
                v_out[s, :, full(t)] = w_keep[s, :, full(t)] + dot3(
                    (a_h[...], a_l[...]), (cov_h[:, full(t)], cov_l[:, full(t)])
                )
                pl.when(goes_down(s))(lambda: v_copy(s, t).start())
                return carry

            lax.fori_loop(0, tiles, last, 0)

        return carry

    lax.fori_loop(0, SPAN + 1, backward, 0)
    spread_out[...] = v_out[0]
    shift_out[...] = vec_out[0]

    @pl.when(tm < n - 1)
    def _():
        for t in range(tiles):
            home_copy(1, t).wait_recv()

    for s in range(SPAN + 1):
        if s > 0:
            pl.when(goes_down(s))(lambda s=s: vec_copy(s).wait_send())
        for t in range(tiles):
            if s < SPAN:
                pl.when(goes_up(s))(lambda s=s, t=t: x_copy(s, t).wait_send())
            if s > 0:
                pl.when(goes_home(s))(lambda s=s, t=t: home_copy(s, t).wait_send())
                pl.when(goes_down(s))(lambda s=s, t=t: v_copy(s, t).wait_send())


def body(n, n_row, covariance, precision, band_weight, band_offset, prior_mean, innovation, seen_sites):
    rows, columns = covariance.shape[1:]
    tiles = columns // TILE
    window = TILE + 2 * EDGE
    steps = SPAN + 1
    block = lambda *lead: pltpu.VMEM(lead + (rows, columns), F32)
    whole = lambda kind: pltpu.VMEM((columns, columns), kind)
    vec = lambda *lead: pltpu.VMEM(lead + (VEC, rows), F32)
    padded = columns + 2 * EDGE
    copies = max(7, n_row - 1)
    dma = lambda *shape: pltpu.SemaphoreType.DMA(shape)
    vmem = pl.BlockSpec(memory_space=pltpu.VMEM)
    gain, shift, spread = pl.pallas_call(
        functools.partial(kernel, n, n_row),
        out_shape=(
            jax.ShapeDtypeStruct((rows, columns), F32),
            jax.ShapeDtypeStruct((VEC, rows), F32),
            jax.ShapeDtypeStruct((rows, columns), F32),
        ),
        in_specs=[pl.BlockSpec(memory_space=pltpu.SMEM)] + [vmem] * 6,
        out_specs=(vmem, vmem, vmem),
        scratch_shapes=[
            whole(F32), whole(F32),
            whole(BF16), whole(BF16), whole(BF16), whole(BF16),
            pltpu.VMEM((tiles, window, TILE), BF16), pltpu.VMEM((tiles, window, TILE), BF16),
            block(SPAN), block(steps), block(steps), block(steps), block(steps),
            pltpu.VMEM((rows, columns), BF16), pltpu.VMEM((rows, columns), BF16),
            pltpu.VMEM((rows, padded), BF16), pltpu.VMEM((rows, padded), BF16),
            block(), pltpu.VMEM((rows, padded), F32),
            vec(n_row),
            pltpu.VMEM((VEC, padded), BF16), pltpu.VMEM((VEC, padded), BF16),
            pltpu.VMEM((VEC, columns), BF16), pltpu.VMEM((VEC, columns), BF16),
            vec(steps), vec(steps), vec(steps),
            dma(2, copies), dma(2, copies), dma(n_row - 1), dma(n_row - 1),
            dma(SPAN, tiles), dma(SPAN, tiles), dma(steps, tiles), dma(tiles),
            dma(steps, tiles), dma(steps, tiles), dma(steps), dma(steps),
        ],
        compiler_params=pltpu.CompilerParams(
            collective_id=0, has_side_effects=True, vmem_limit_bytes=58 * 2**20
        ),
        cost_estimate=pl.CostEstimate(
            flops=2 * 54 * rows * columns * columns, bytes_accessed=16 * rows * columns,
            transcendentals=0,
        ),
    )(
        band_offset,
        covariance[0],
        precision[0],
        band_weight[0],
        jnp.broadcast_to(prior_mean, (VEC, rows)),
        jnp.broadcast_to(innovation, (VEC, innovation.shape[1])),
        seen_sites[0][:, None],
    )
    return gain[None], shift[:1], spread[None]


def solution(mesh):
    in_specs = (
        P("tm", "row", None),
        P("tm", "row", None),
        P("tm", None, None),
        P("tm", None),
        P("tm", "row"),
        P("tm", None),
        P("tm", None),
    )
    out_specs = (P("tm", "row", None), P("tm", "row"), P("tm", "row", None))
    return jax.shard_map(
        functools.partial(body, mesh.shape["tm"], mesh.shape["row"]),
        mesh=mesh, in_specs=in_specs, out_specs=out_specs, check_vma=False,
    )
```

```python
import functools

import jax
import jax.numpy as jnp
from jax import lax
from jax.experimental import pallas as pl
from jax.experimental.pallas import tpu as pltpu
from jax.sharding import PartitionSpec as P

NBAND = 5
REACH = 64
SPAN = 3
TILE = 256
EDGE = 128
VEC = 16

MESH = pl.DeviceIdType.MESH
F32 = jnp.float32
BF16 = jnp.bfloat16


def split(value):
    high = value.astype(BF16)
    return high, (value - high.astype(F32)).astype(BF16)


def dot3(left, right):
    (lh, ll), (rh, rl) = left, right
    one = functools.partial(jnp.dot, preferred_element_type=F32)
    return one(lh, rh) + (one(lh, rl) + one(ll, rh))


def dot3t(left, right):
    (lh, ll), (rh, rl) = left, right

    def one(a, b):
        return lax.dot_general(a, b, (((1,), (1,)), ((), ())), preferred_element_type=F32)

    return one(lh, rh) + (one(lh, rl) + one(ll, rh))


def kernel(
    n, n_row,
    offsets, cov_rows, inv_rows, weights, prior, innovation, seen,
    gain_out, shift_out, spread_out,
    land, rows_two, bands, cov_h, cov_l, inv_h, inv_l, ft_h, ft_l,
    x_in, x_keep, w_keep, v_in, v_out, a_h, a_l, pad_h, pad_l, acc, pad_acc,
    prior_all, means, f_h, f_l, h_h, h_l, part, vec_in, vec_out,
    g_send, g_recv, r_send, r_recv, s_send, s_recv, p_send, p_recv,
    x_send, x_recv, home_send, home_recv, v_send, v_recv, vec_send, vec_recv,
):
    tm = lax.axis_index("tm")
    row = lax.axis_index("row")
    rows, columns = cov_rows.shape
    tiles = columns // TILE
    even = lax.rem(tm, 2) == 0
    odd = lax.rem(tm, 2) == 1

    def at(index, size):
        return pl.ds(pl.multiple_of(index * size, size), size)

    def remote(src, dst, send, recv, to_tm, to_row):
        return pltpu.make_async_remote_copy(
            src_ref=src, dst_ref=dst, send_sem=send, recv_sem=recv,
            device_id=(to_tm, to_row), device_id_type=MESH,
        )

    barrier = pltpu.get_barrier_semaphore()

    def greet(t, r):
        pl.semaphore_signal(barrier, inc=1, device_id=(t, r), device_id_type=MESH)

    for d in range(1, n_row):
        greet(tm, lax.rem(row + d, n_row))
    for d in range(1, SPAN + 1):
        pl.when(tm + d < n)(lambda d=d: greet(tm + d, row))
        pl.when(tm - d >= 0)(lambda d=d: greet(tm - d, row))
    pl.semaphore_wait(
        barrier, n_row - 1 + jnp.minimum(tm, SPAN) + jnp.minimum(n - 1 - tm, SPAN)
    )

    twin = even & (tm >= 2) & (tm + 2 < n)
    lends = even & (tm >= 4)

    def valid(s):
        last = (odd & (tm >= SPAN)) | twin
        return ((s < SPAN) & (tm >= s)) | ((s == SPAN) & last)

    def goes_on(s):
        return valid(s) & (s < SPAN) & (tm + 1 < n)

    def goes_home(s):
        return valid(s) & (s > 0) & ((s == SPAN) | (tm == n - 1))

    def goes_back(s):
        return valid(s) & (s > 0)

    def chosen(s):
        return jnp.where((s == SPAN) & even, 1, 0)

    square = n_row == 4 and rows == TILE
    half = rows // 2
    if square:
        x, y = lax.rem(row, 2), row // 2
        r1, r2, r3 = 2 * y + 1 - x, 2 * (1 - y) + x, 2 * (1 - y) + 1 - x
        every, low, top = pl.ds(0, rows), pl.ds(0, half), pl.ds(half, half)
        right = pl.ds(pl.multiple_of(row * rows + half, half), half)
        right3 = pl.ds(pl.multiple_of(r3 * rows + half, half), half)
        plan = []
        for slot, to in enumerate((r1, r2, r3)):
            plan.append((to, slot, low, at(row, rows), every))
            plan.append((to, slot, top, right, top))
        plan.append((r1, 3, every, at(r2, rows), every))
        plan.append((r2, 4, every, at(r1, rows), every))
        plan.append((r1, 5, low, at(r3, rows), every))
        plan.append((r2, 6, every, right3, low))
    else:
        every = pl.ds(0, rows)
        wide = pl.ds(0, columns)
        plan = [
            (lax.rem(row + d, n_row), d - 1, every, wide, wide) for d in range(1, n_row)
        ]

    def gather(m, src):
        return [
            remote(
                src.at[rsl, csl], land.at[0, m, slot, rsl, dsl],
                g_send.at[m, c], g_recv.at[m, c], tm, to,
            )
            for c, (to, slot, rsl, csl, dsl) in enumerate(plan)
        ]

    def lend(m):
        return [
            remote(
                land.at[0, m, slot, rsl, dsl], land.at[1, m, slot, rsl, dsl],
                r_send.at[m, c], r_recv.at[m, c], tm - 2, row,
            )
            for c, (to, slot, rsl, csl, dsl) in enumerate(plan)
        ]

    def small(c, src, dst):
        return remote(src, dst, s_send.at[c], s_recv.at[c], tm - 2, row)

    lend_rows = [
        small(0, inv_rows, rows_two.at[0]), small(1, cov_rows, rows_two.at[1])
    ]
    lend_bands = small(2, bands.at[0], bands.at[1])
    lend_means = small(3, means.at[0], means.at[1])

    def fill(which, m, src, high, low_part):
        def put(rsl, csl, value):
            h, l = split(value)
            high[which, rsl, csl] = h
            low_part[which, rsl, csl] = l

        put(at(row, rows), pl.ds(0, columns), src[...])
        if not square:
            for d in range(1, n_row):
                owner = lax.rem(row + n_row - d, n_row)
                put(at(owner, rows), pl.ds(0, columns), land[which, m, d - 1])
            return
        for slot, r in enumerate((r1, r2, r3)):
            put(at(r, rows), at(row, rows), src[:, at(r, rows)].T)
            upper = pl.ds(pl.multiple_of(r * rows, half), half)
            lower = pl.ds(pl.multiple_of(r * rows + half, half), half)
            put(upper, at(r, rows), land[which, m, slot, :half, :])
            put(lower, lower, land[which, m, slot, half:, half:])
            put(lower, upper, land[which, m, slot, :half, half:].T)
        for slot, r in ((3, r1), (4, r2)):
            block = land[which, m, slot]
            put(at(r, rows), at(r3, rows), block)
            put(at(r3, rows), at(r, rows), block.T)
        upper = pl.ds(pl.multiple_of(r1 * rows, half), half)
        lower = pl.ds(pl.multiple_of(r1 * rows + half, half), half)
        block = land[which, m, 5, :half, :]
        put(upper, at(r2, rows), block)
        put(at(r2, rows), upper, block.T)
        block = land[which, m, 6, :, :half]
        put(at(r2, rows), lower, block)
        put(lower, at(r2, rows), block.T)

    inv_copies = gather(0, inv_rows)
    cov_copies = gather(1, cov_rows)
    for c in inv_copies:
        c.start()

    bands[0] = jnp.zeros(bands.shape[1:], F32)
    bands[0, :NBAND, :] = weights[...]
    for b in range(NBAND):
        bands[0, 8 + b : 9 + b, :] = jnp.full((1, columns), offsets[0, b].astype(F32))

    @pl.when(lends)
    def _():
        lend_bands.start()
        for c in lend_rows:
            c.start()

    vec_out[0] = jnp.broadcast_to(prior[...], (VEC, rows))
    prior_all[row] = vec_out[0]
    prior_copies = [
        remote(
            vec_out.at[0], prior_all.at[row], p_send.at[d - 1], p_recv.at[d - 1],
            tm, lax.rem(row + d, n_row),
        )
        for d in range(1, n_row)
    ]
    for c in prior_copies:
        c.start()

    window = TILE + 2 * EDGE

    def windows(which):
        apart = lax.broadcasted_iota(jnp.int32, (window, TILE), 0) - (
            lax.broadcasted_iota(jnp.int32, (window, TILE), 1) + EDGE
        )
        apart = apart.astype(F32)
        for t in range(tiles):
            cols = slice(t * TILE, (t + 1) * TILE)
            total = jnp.zeros((window, TILE), F32)
            for b in range(NBAND):
                hit = apart == bands[which, 8 + b : 9 + b, cols]
                total = total + jnp.where(hit, bands[which, b : b + 1, cols], 0.0)
            h, l = split(total)
            ft_h[which, t] = h
            ft_l[which, t] = l

    windows(0)

    zeros = jnp.zeros((rows, EDGE), BF16)
    for ref in (pad_h, pad_l):
        ref[:, :EDGE] = zeros
        ref[:, EDGE + columns :] = zeros

    def full(t):
        return pl.ds(pl.multiple_of(t * TILE, TILE), TILE)

    def x_copy(s, t):
        to = jnp.where((s == SPAN - 1) & odd, tm - 1, tm + 1)
        return remote(
            x_keep.at[s, :, full(t)], x_in.at[s, :, full(t)],
            x_send.at[s, t], x_recv.at[s, t], to, row,
        )

    def home_copy(s, t):
        to = tm - jnp.where((s == SPAN) & even, 1, s)
        return remote(
            x_keep.at[s, :, full(t)], gain_out.at[:, full(t)],
            home_send.at[s, t], home_recv.at[t], to, row,
        )

    def back_to(s):
        return jnp.where((s == SPAN) & even, tm + 1, tm - 1)

    def v_copy(s, t):
        return remote(
            v_out.at[s - 1, :, full(t)], v_in.at[s - 1, :, full(t)],
            v_send.at[s, t], v_recv.at[s, t], back_to(s), row,
        )

    def vec_copy(s):
        return remote(
            vec_out.at[s], vec_in.at[s], vec_send.at[s], vec_recv.at[s], back_to(s), row
        )

    def band_step(s, which):
        h, l = split(w_keep[s])
        pad_h[:, EDGE : EDGE + columns] = h
        pad_l[:, EDGE : EDGE + columns] = l
        for t in range(tiles):
            wide = slice(t * TILE, t * TILE + window)
            h, l = split(
                dot3((pad_h[:, wide], pad_l[:, wide]), (ft_h[which, t], ft_l[which, t]))
            )
            a_h[:, t * TILE : (t + 1) * TILE] = h
            a_l[:, t * TILE : (t + 1) * TILE] = l

    def gain_step(s, which):
        def one(t, carry):
            x_keep[s, :, full(t)] = dot3(
                (a_h[...], a_l[...]), (inv_h[which, :, full(t)], inv_l[which, :, full(t)])
            )
            pl.when(goes_on(s))(lambda: x_copy(s, t).start())
            early = goes_home(s) & ((s < SPAN) | (t < tiles // 2))
            pl.when(early)(lambda: home_copy(s, t).start())
            return carry

        lax.fori_loop(0, tiles, one, 0)

    w_keep[0] = cov_rows[...]
    band_step(0, 0)
    for c in inv_copies:
        c.wait_send()
    for c in cov_copies:
        c.start()
    for c in inv_copies:
        c.wait_recv()

    @pl.when(lends)
    def _():
        for c in lend(0):
            c.start()

    fill(0, 0, inv_rows, inv_h, inv_l)
    gain_step(0, 0)

    @pl.when(tm == n - 1)
    def _():
        gain_out[...] = x_keep[0]

    count = seen.shape[1]
    spots = jnp.broadcast_to(seen[...].astype(F32), (count, count)).T
    lanes = lax.broadcasted_iota(jnp.int32, (count, count), 1).astype(F32)
    matches = jnp.concatenate(
        [
            jnp.where(lanes + float(c * count) == spots, 1.0, 0.0)
            for c in range(columns // count)
        ],
        axis=1,
    ).astype(BF16)
    values = jnp.broadcast_to(innovation[...], (VEC, count))
    first, second = split(values)
    third = (values - first.astype(F32) - second.astype(F32)).astype(BF16)
    total = jnp.zeros((VEC, columns), F32)
    for piece in (third, second, first):
        total = total + jnp.dot(piece, matches, preferred_element_type=F32)
    pulled = split(total)
    own = vec_out[0] + dot3t(pulled, split(cov_rows[...]))
    for c in prior_copies:
        c.wait()
    for c in cov_copies:
        c.wait()

    @pl.when(lends)
    def _():
        for c in lend(1):
            c.start()

    fill(0, 1, cov_rows, cov_h, cov_l)
    inside = slice(EDGE, EDGE + columns)

    def cut_means(which):
        zeros = jnp.zeros((VEC, EDGE), BF16)
        h, l = split(means[which, 0])
        for ref, value in ((f_h, h), (f_l, l)):
            ref[which, :, :EDGE] = zeros
            ref[which, :, EDGE + columns :] = zeros
            ref[which, :, inside] = value

    def cut_moved(which):
        h, l = split(means[which, 1])
        h_h[which] = h
        h_l[which] = l

    def filtered():
        prior_row = jnp.concatenate([prior_all[r] for r in range(n_row)], axis=1)
        for t in range(tiles):
            cols = slice(t * TILE, (t + 1) * TILE)
            means[0, 0, :, cols] = prior_row[:, cols] + dot3(
                pulled, (cov_h[0, :, cols], cov_l[0, :, cols])
            )
        cut_means(0)
        for t in range(tiles):
            wide = slice(t * TILE, t * TILE + window)
            means[0, 1, :, t * TILE : (t + 1) * TILE] = dot3(
                (f_h[0, :, wide], f_l[0, :, wide]), (ft_h[0, t], ft_l[0, t])
            )
        cut_moved(0)
        pl.when(lends)(lambda: lend_means.start())

    def moved_part(s, which):
        return dot3t((h_h[which], h_l[which]), split(x_keep[s]))

    def forward(s, carry):
        which = chosen(s)

        @pl.when(twin & (s == SPAN))
        def _():
            for c in lend(1):
                c.wait_recv()
            lend_rows[1].wait_recv()
            fill(1, 1, rows_two.at[1], cov_h, cov_l)
            lend_means.wait_recv()
            cut_means(1)
            cut_moved(1)

        @pl.when(valid(s))
        def _():
            w_keep[s] = jnp.zeros((rows, columns), F32)

            def one(t, carry):
                x_copy(s - 1, t).wait_recv()
                piece = split(x_in[s - 1, :, full(t)])
                for c in range(0, columns, 2 * TILE):
                    cols = slice(c, c + 2 * TILE)
                    w_keep[s, :, cols] += dot3(
                        piece, (cov_h[which, full(t), cols], cov_l[which, full(t), cols])
                    )
                return carry

            lax.fori_loop(0, tiles, one, 0)
            band_step(s, which)
            gain_step(s, which)

        @pl.when(s == 1)
        def _():
            filtered()
            part[0] = own - moved_part(0, 0)

        @pl.when(valid(s))
        def _():
            part[s] = dot3t(
                (f_h[which, :, inside], f_l[which, :, inside]), split(x_in[s - 1])
            ) - moved_part(s, which)

        @pl.when(twin & (s == 1))
        def _():
            for c in lend(0):
                c.wait_recv()
            lend_rows[0].wait_recv()
            lend_bands.wait_recv()
            windows(1)
            fill(1, 0, rows_two.at[0], inv_h, inv_l)

        return carry

    lax.fori_loop(1, SPAN + 1, forward, 0)

    def backward(i, carry):
        s = SPAN - i
        which = chosen(s)

        @pl.when(valid(s))
        def _():
            acc[...] = -x_keep[s]
            vec_out[s] = part[s]

            @pl.when((s < SPAN) & (tm < n - 1))
            def _():
                def one(t, carry):
                    v_copy(s + 1, t).wait_recv()
                    piece = split(v_in[s, :, full(t)])
                    for c in range(0, columns, 2 * TILE):
                        cols = slice(c, c + 2 * TILE)
                        acc[:, cols] += dot3(
                            piece, (inv_h[0, full(t), cols], inv_l[0, full(t), cols])
                        )
                    return carry

                lax.fori_loop(0, tiles, one, 0)
                vec_copy(s + 1).wait_recv()
                vec_out[s] += vec_in[s + 1]

            pl.when(goes_back(s))(lambda: vec_copy(s).start())
            pad_acc[...] = jnp.zeros(pad_acc.shape, F32)
            for t in range(tiles):
                wide = slice(t * TILE, t * TILE + window)
                piece = split(acc[:, t * TILE : (t + 1) * TILE])
                pad_acc[:, wide] += dot3t(piece, (ft_h[which, t], ft_l[which, t]))
            h, l = split(pad_acc[:, inside])
            a_h[...] = h
            a_l[...] = l

            def last(t, carry):
                value = w_keep[s, :, full(t)] + dot3(
                    (a_h[...], a_l[...]), (cov_h[which, :, full(t)], cov_l[which, :, full(t)])
                )

                @pl.when(s > 0)
                def _():
                    v_out[s - 1, :, full(t)] = value
                    v_copy(s, t).start()

                @pl.when(s == 0)
                def _():
                    spread_out[:, full(t)] = value

                return carry

            lax.fori_loop(0, tiles, last, 0)

        @pl.when((s == 1) & valid(SPAN))
        def _():
            for t in range(tiles // 2, tiles):
                home_copy(SPAN, t).start()

        return carry

    lax.fori_loop(0, SPAN + 1, backward, 0)
    shift_out[...] = vec_out[0, :1, :]

    @pl.when(tm < n - 1)
    def _():
        for t in range(tiles):
            home_copy(1, t).wait_recv()

    @pl.when(lends)
    def _():
        for c in lend_rows + [lend_bands, lend_means] + lend(0) + lend(1):
            c.wait_send()

    for s in range(SPAN + 1):
        if s > 0:
            pl.when(goes_back(s))(lambda s=s: vec_copy(s).wait_send())
        for t in range(tiles):
            if s < SPAN:
                pl.when(goes_on(s))(lambda s=s, t=t: x_copy(s, t).wait_send())
            if s > 0:
                pl.when(goes_home(s))(lambda s=s, t=t: home_copy(s, t).wait_send())
                pl.when(goes_back(s))(lambda s=s, t=t: v_copy(s, t).wait_send())


def body(n, n_row, covariance, precision, band_weight, band_offset, prior_mean, innovation, seen_sites):
    rows, columns = covariance.shape[1:]
    tiles = columns // TILE
    window = TILE + 2 * EDGE
    steps = SPAN + 1
    square = n_row == 4 and rows == TILE
    copies = 10 if square else n_row - 1
    slots = (7, rows, rows) if square else (n_row - 1, rows, columns)
    block = lambda *lead: pltpu.VMEM(lead + (rows, columns), F32)
    whole = pltpu.VMEM((2, columns, columns), BF16)
    vec = lambda *lead: pltpu.VMEM(lead + (VEC, rows), F32)
    padded = columns + 2 * EDGE
    dma = lambda *shape: pltpu.SemaphoreType.DMA(shape)
    vmem = pl.BlockSpec(memory_space=pltpu.VMEM)
    gain, shift, spread = pl.pallas_call(
        functools.partial(kernel, n, n_row),
        out_shape=(
            jax.ShapeDtypeStruct((rows, columns), F32),
            jax.ShapeDtypeStruct((1, rows), F32),
            jax.ShapeDtypeStruct((rows, columns), F32),
        ),
        in_specs=[pl.BlockSpec(memory_space=pltpu.SMEM)] + [vmem] * 6,
        out_specs=(vmem, vmem, vmem),
        scratch_shapes=[
            pltpu.VMEM((2, 2) + slots, F32), block(2), pltpu.VMEM((2, 16, columns), F32),
            whole, whole, whole, whole,
            pltpu.VMEM((2, tiles, window, TILE), BF16), pltpu.VMEM((2, tiles, window, TILE), BF16),
            block(SPAN), block(steps), block(steps), block(SPAN), block(SPAN),
            pltpu.VMEM((rows, columns), BF16), pltpu.VMEM((rows, columns), BF16),
            pltpu.VMEM((rows, padded), BF16), pltpu.VMEM((rows, padded), BF16),
            block(), pltpu.VMEM((rows, padded), F32),
            vec(n_row), pltpu.VMEM((2, 2, VEC, columns), F32),
            pltpu.VMEM((2, VEC, padded), BF16), pltpu.VMEM((2, VEC, padded), BF16),
            pltpu.VMEM((2, VEC, columns), BF16), pltpu.VMEM((2, VEC, columns), BF16),
            vec(steps), vec(steps), vec(steps),
            dma(2, copies), dma(2, copies), dma(2, copies), dma(2, copies), dma(4), dma(4),
            dma(n_row - 1), dma(n_row - 1),
            dma(SPAN, tiles), dma(SPAN, tiles), dma(steps, tiles), dma(tiles),
            dma(steps, tiles), dma(steps, tiles), dma(steps), dma(steps),
        ],
        compiler_params=pltpu.CompilerParams(
            collective_id=0, has_side_effects=True, vmem_limit_bytes=62 * 2**20
        ),
        cost_estimate=pl.CostEstimate(
            flops=2 * 54 * rows * columns * columns, bytes_accessed=16 * rows * columns,
            transcendentals=0,
        ),
    )(
        band_offset, covariance[0], precision[0], band_weight[0],
        prior_mean, innovation, seen_sites,
    )
    return gain[None], shift, spread[None]


def solution(mesh):
    in_specs = (
        P("tm", "row", None),
        P("tm", "row", None),
        P("tm", None, None),
        P("tm", None),
        P("tm", "row"),
        P("tm", None),
        P("tm", None),
    )
    out_specs = (P("tm", "row", None), P("tm", "row"), P("tm", "row", None))
    return jax.shard_map(
        functools.partial(body, mesh.shape["tm"], mesh.shape["row"]),
        mesh=mesh, in_specs=in_specs, out_specs=out_specs, check_vma=False,
    )
```

```python
import functools

import jax
import jax.numpy as jnp
from jax import lax
from jax.experimental import pallas as pl
from jax.experimental.pallas import tpu as pltpu
from jax.sharding import PartitionSpec as P

NBAND = 5
REACH = 64
SPAN = 3
TILE = 256
EDGE = 128
VEC = 16

MESH = pl.DeviceIdType.MESH
F32 = jnp.float32
BF16 = jnp.bfloat16


def split(value):
    high = value.astype(BF16)
    return high, (value - high.astype(F32)).astype(BF16)


def stack(value):
    return jnp.concatenate(split(value), axis=0)


def dot3(left, right):
    high, low = right
    one = functools.partial(jnp.dot, preferred_element_type=F32)
    count = left.shape[0] // 2
    both = one(left, high)
    return both[:count] + (both[count:] + one(left[:count], low))


def dot3t(left, right):
    high, low = right

    def one(a, b):
        return lax.dot_general(a, b, (((1,), (1,)), ((), ())), preferred_element_type=F32)

    count = left.shape[0] // 2
    both = one(left, high)
    return both[:count] + (both[count:] + one(left[:count], low))


def kernel(
    n, n_row,
    offsets, cov_rows, inv_rows, weights, prior, innovation, seen,
    gain_out, shift_out, spread_out,
    land, rows_two, bands, cov_h, cov_l, inv_h, inv_l, ft_h, ft_l,
    x_in, x_keep, w_keep, v_in, v_out, a_hl, pad_hl, acc, pad_acc,
    prior_all, means, f_hl, h_hl, part, vec_in, vec_out,
    g_send, g_recv, r_send, r_recv, s_send, s_recv, p_send, p_recv,
    x_send, x_recv, home_send, home_recv, v_send, v_recv, vec_send, vec_recv,
):
    tm = lax.axis_index("tm")
    row = lax.axis_index("row")
    rows, columns = cov_rows.shape
    tiles = columns // TILE
    even = lax.rem(tm, 2) == 0
    odd = lax.rem(tm, 2) == 1

    def at(index, size):
        return pl.ds(pl.multiple_of(index * size, size), size)

    def remote(src, dst, send, recv, to_tm, to_row):
        return pltpu.make_async_remote_copy(
            src_ref=src, dst_ref=dst, send_sem=send, recv_sem=recv,
            device_id=(to_tm, to_row), device_id_type=MESH,
        )

    barrier = pltpu.get_barrier_semaphore()

    def greet(t, r):
        pl.semaphore_signal(barrier, inc=1, device_id=(t, r), device_id_type=MESH)

    for d in range(1, n_row):
        greet(tm, lax.rem(row + d, n_row))
    for d in range(1, SPAN + 1):
        pl.when(tm + d < n)(lambda d=d: greet(tm + d, row))
        pl.when(tm - d >= 0)(lambda d=d: greet(tm - d, row))
    pl.semaphore_wait(
        barrier, n_row - 1 + jnp.minimum(tm, SPAN) + jnp.minimum(n - 1 - tm, SPAN)
    )

    twin = even & (tm >= 2) & (tm + 2 < n)
    lends = even & (tm >= 4)

    def valid(s):
        last = (odd & (tm >= SPAN)) | twin
        return ((s < SPAN) & (tm >= s)) | ((s == SPAN) & last)

    def goes_on(s):
        return valid(s) & (s < SPAN) & (tm + 1 < n)

    def goes_home(s):
        return valid(s) & (s > 0) & ((s == SPAN) | (tm == n - 1))

    def goes_back(s):
        return valid(s) & (s > 0)

    def chosen(s):
        return jnp.where((s == SPAN) & even, 1, 0)

    square = n_row == 4 and rows == TILE
    half = rows // 2
    if square:
        x, y = lax.rem(row, 2), row // 2
        r1, r2, r3 = 2 * y + 1 - x, 2 * (1 - y) + x, 2 * (1 - y) + 1 - x
        every, low, top = pl.ds(0, rows), pl.ds(0, half), pl.ds(half, half)
        right = pl.ds(pl.multiple_of(row * rows + half, half), half)
        right3 = pl.ds(pl.multiple_of(r3 * rows + half, half), half)
        plan = []
        for slot, to in enumerate((r1, r2, r3)):
            plan.append((to, slot, low, at(row, rows), every))
            plan.append((to, slot, top, right, top))
        plan.append((r1, 3, every, at(r2, rows), every))
        plan.append((r2, 4, every, at(r1, rows), every))
        plan.append((r1, 5, low, at(r3, rows), every))
        plan.append((r2, 6, every, right3, low))
    else:
        every = pl.ds(0, rows)
        wide = pl.ds(0, columns)
        plan = [
            (lax.rem(row + d, n_row), d - 1, every, wide, wide) for d in range(1, n_row)
        ]

    def gather(m, src):
        return [
            remote(
                src.at[rsl, csl], land.at[0, m, slot, rsl, dsl],
                g_send.at[m, c], g_recv.at[m, c], tm, to,
            )
            for c, (to, slot, rsl, csl, dsl) in enumerate(plan)
        ]

    def lend(m):
        return [
            remote(
                land.at[0, m, slot, rsl, dsl], land.at[1, m, slot, rsl, dsl],
                r_send.at[m, c], r_recv.at[m, c], tm - 2, row,
            )
            for c, (to, slot, rsl, csl, dsl) in enumerate(plan)
        ]

    def small(c, src, dst):
        return remote(src, dst, s_send.at[c], s_recv.at[c], tm - 2, row)

    lend_rows = [
        small(0, inv_rows, rows_two.at[0]), small(1, cov_rows, rows_two.at[1])
    ]
    lend_bands = small(2, bands.at[0], bands.at[1])
    lend_means = small(3, means.at[0], means.at[1])

    def putter(which, high, low_part):
        def put(rsl, csl, value):
            h, l = split(value)
            high[which, rsl, csl] = h
            low_part[which, rsl, csl] = l

        return put

    def fill_own(which, src, high, low_part):
        put = putter(which, high, low_part)
        put(at(row, rows), pl.ds(0, columns), src[...])
        if square:
            for r in (r1, r2, r3):
                put(at(r, rows), at(row, rows), src[:, at(r, rows)].T)

    def fill_slots(which, m, copies, high, low_part, on=None):
        put = putter(which, high, low_part)
        for slot in range(7 if square else n_row - 1):
            for c, entry in enumerate(plan):
                if entry[1] == slot:
                    copies[c].wait_recv()
                    if on is not None:
                        pl.when(lends)(lambda c=c: on[c].start())
            if not square:
                owner = lax.rem(row + n_row - 1 - slot, n_row)
                put(at(owner, rows), pl.ds(0, columns), land[which, m, slot])
            elif slot < 3:
                r = (r1, r2, r3)[slot]
                upper = pl.ds(pl.multiple_of(r * rows, half), half)
                lower = pl.ds(pl.multiple_of(r * rows + half, half), half)
                put(upper, at(r, rows), land[which, m, slot, :half, :])
                put(lower, lower, land[which, m, slot, half:, half:])
                put(lower, upper, land[which, m, slot, :half, half:].T)
            elif slot < 5:
                r = r1 if slot == 3 else r2
                block = land[which, m, slot]
                put(at(r, rows), at(r3, rows), block)
                put(at(r3, rows), at(r, rows), block.T)
            else:
                upper = pl.ds(pl.multiple_of(r1 * rows, half), half)
                lower = pl.ds(pl.multiple_of(r1 * rows + half, half), half)
                if slot == 5:
                    block = land[which, m, 5, :half, :]
                    put(upper, at(r2, rows), block)
                    put(at(r2, rows), upper, block.T)
                else:
                    block = land[which, m, 6, :, :half]
                    put(at(r2, rows), lower, block)
                    put(lower, at(r2, rows), block.T)

    inv_copies = gather(0, inv_rows)
    cov_copies = gather(1, cov_rows)
    for c in inv_copies:
        c.start()

    bands[0] = jnp.zeros(bands.shape[1:], F32)
    bands[0, :NBAND, :] = weights[...]
    for b in range(NBAND):
        bands[0, 8 + b : 9 + b, :] = jnp.full((1, columns), offsets[0, b].astype(F32))

    @pl.when(lends)
    def _():
        lend_bands.start()
        for c in lend_rows:
            c.start()

    vec_out[0] = jnp.broadcast_to(prior[...], (VEC, rows))
    prior_all[row] = vec_out[0]
    prior_copies = [
        remote(
            vec_out.at[0], prior_all.at[row], p_send.at[d - 1], p_recv.at[d - 1],
            tm, lax.rem(row + d, n_row),
        )
        for d in range(1, n_row)
    ]
    for c in prior_copies:
        c.start()

    window = TILE + 2 * EDGE

    def windows(which):
        apart = lax.broadcasted_iota(jnp.int32, (window, TILE), 0) - (
            lax.broadcasted_iota(jnp.int32, (window, TILE), 1) + EDGE
        )
        apart = apart.astype(F32)
        for t in range(tiles):
            cols = slice(t * TILE, (t + 1) * TILE)
            total = jnp.zeros((window, TILE), F32)
            for b in range(NBAND):
                hit = apart == bands[which, 8 + b : 9 + b, cols]
                total = total + jnp.where(hit, bands[which, b : b + 1, cols], 0.0)
            h, l = split(total)
            ft_h[which, t] = h
            ft_l[which, t] = l

    windows(0)

    zeros = jnp.zeros((rows, EDGE), BF16)
    for first in (0, rows):
        pad_hl[first : first + rows, :EDGE] = zeros
        pad_hl[first : first + rows, EDGE + columns :] = zeros

    def full(t):
        return pl.ds(pl.multiple_of(t * TILE, TILE), TILE)

    def x_copy(s, t):
        to = jnp.where((s == SPAN - 1) & odd, tm - 1, tm + 1)
        return remote(
            x_keep.at[s, :, full(t)], x_in.at[s, :, full(t)],
            x_send.at[s, t], x_recv.at[s, t], to, row,
        )

    def home_copy(s, t):
        to = tm - jnp.where((s == SPAN) & even, 1, s)
        return remote(
            x_keep.at[s, :, full(t)], gain_out.at[:, full(t)],
            home_send.at[s, t], home_recv.at[t], to, row,
        )

    def back_to(s):
        return jnp.where((s == SPAN) & even, tm + 1, tm - 1)

    def v_copy(s, t):
        return remote(
            v_out.at[s - 1, :, full(t)], v_in.at[s - 1, :, full(t)],
            v_send.at[s, t], v_recv.at[s, t], back_to(s), row,
        )

    def vec_copy(s):
        return remote(
            vec_out.at[s], vec_in.at[s], vec_send.at[s], vec_recv.at[s], back_to(s), row
        )

    pair = 2 * TILE

    def two(c):
        return pl.ds(pl.multiple_of(c * pair, pair), pair)

    def band_step(s, which):
        h, l = split(w_keep[s])
        pad_hl[:rows, EDGE : EDGE + columns] = h
        pad_hl[rows:, EDGE : EDGE + columns] = l
        for t in range(tiles):
            wide = slice(t * TILE, t * TILE + window)
            cols = slice(t * TILE, (t + 1) * TILE)
            h, l = split(dot3(pad_hl[:, wide], (ft_h[which, t], ft_l[which, t])))
            a_hl[:rows, cols] = h
            a_hl[rows:, cols] = l

    def gain_step(s, which):
        def one(c, carry):
            x_keep[s, :, two(c)] = dot3(
                a_hl[...], (inv_h[which, :, two(c)], inv_l[which, :, two(c)])
            )
            for i in range(2):
                t = 2 * c + i
                pl.when(goes_on(s))(lambda t=t: x_copy(s, t).start())
                early = goes_home(s) & ((s < SPAN) | (t < tiles // 2))
                pl.when(early)(lambda t=t: home_copy(s, t).start())
            return carry

        lax.fori_loop(0, tiles // 2, one, 0)

    w_keep[0] = cov_rows[...]
    band_step(0, 0)
    fill_own(0, inv_rows, inv_h, inv_l)
    fill_own(0, cov_rows, cov_h, cov_l)
    for c in inv_copies:
        c.wait_send()
    for c in cov_copies:
        c.start()
    fill_slots(0, 0, inv_copies, inv_h, inv_l, lend(0))
    gain_step(0, 0)

    @pl.when(tm == n - 1)
    def _():
        gain_out[...] = x_keep[0]

    count = seen.shape[1]
    spots = jnp.broadcast_to(seen[...].astype(F32), (count, count)).T
    lanes = lax.broadcasted_iota(jnp.int32, (count, count), 1).astype(F32)
    matches = jnp.concatenate(
        [
            jnp.where(lanes + float(c * count) == spots, 1.0, 0.0)
            for c in range(columns // count)
        ],
        axis=1,
    ).astype(BF16)
    values = jnp.broadcast_to(innovation[...], (VEC, count))
    first, second = split(values)
    third = (values - first.astype(F32) - second.astype(F32)).astype(BF16)
    total = jnp.zeros((VEC, columns), F32)
    for piece in (third, second, first):
        total = total + jnp.dot(piece, matches, preferred_element_type=F32)
    pulled = stack(total)
    own = vec_out[0] + dot3t(pulled, split(cov_rows[...]))
    for c in prior_copies:
        c.wait()
    fill_slots(0, 1, cov_copies, cov_h, cov_l, lend(1))
    for c in cov_copies:
        c.wait_send()
    inside = slice(EDGE, EDGE + columns)

    def cut_means(which):
        zeros = jnp.zeros((2 * VEC, EDGE), BF16)
        f_hl[which, :, :EDGE] = zeros
        f_hl[which, :, EDGE + columns :] = zeros
        f_hl[which, :, inside] = stack(means[which, 0])

    def cut_moved(which):
        h_hl[which] = stack(means[which, 1])

    def filtered():
        prior_row = jnp.concatenate([prior_all[r] for r in range(n_row)], axis=1)
        for t in range(tiles):
            cols = slice(t * TILE, (t + 1) * TILE)
            means[0, 0, :, cols] = prior_row[:, cols] + dot3(
                pulled, (cov_h[0, :, cols], cov_l[0, :, cols])
            )
        cut_means(0)
        for t in range(tiles):
            wide = slice(t * TILE, t * TILE + window)
            means[0, 1, :, t * TILE : (t + 1) * TILE] = dot3(
                f_hl[0, :, wide], (ft_h[0, t], ft_l[0, t])
            )
        cut_moved(0)
        pl.when(lends)(lambda: lend_means.start())

    def moved_part(s, which):
        return dot3t(h_hl[which], split(x_keep[s]))

    def forward(s, carry):
        which = chosen(s)

        @pl.when(twin & (s == SPAN))
        def _():
            fill_slots(1, 1, lend(1), cov_h, cov_l)
            lend_means.wait_recv()
            cut_means(1)
            cut_moved(1)

        @pl.when(valid(s))
        def _():
            w_keep[s] = jnp.zeros((rows, columns), F32)

            def one(t, carry):
                x_copy(s - 1, t).wait_recv()
                piece = stack(x_in[s - 1, :, full(t)])
                for c in range(0, columns, 2 * TILE):
                    cols = slice(c, c + 2 * TILE)
                    w_keep[s, :, cols] += dot3(
                        piece, (cov_h[which, full(t), cols], cov_l[which, full(t), cols])
                    )
                return carry

            lax.fori_loop(0, tiles, one, 0)
            band_step(s, which)
            gain_step(s, which)

        @pl.when(s == 1)
        def _():
            filtered()
            part[0] = own - moved_part(0, 0)

        @pl.when(valid(s))
        def _():
            part[s] = dot3t(f_hl[which, :, inside], split(x_in[s - 1])) - moved_part(s, which)

        @pl.when(twin & (s == 1))
        def _():
            lend_bands.wait_recv()
            windows(1)
            for c in lend_rows:
                c.wait_recv()
            fill_own(1, rows_two.at[0], inv_h, inv_l)
            fill_own(1, rows_two.at[1], cov_h, cov_l)
            fill_slots(1, 0, lend(0), inv_h, inv_l)

        return carry

    lax.fori_loop(1, SPAN + 1, forward, 0)

    def backward(i, carry):
        s = SPAN - i
        which = chosen(s)

        @pl.when(valid(s))
        def _():
            acc[...] = -x_keep[s]
            vec_out[s] = part[s]

            @pl.when((s < SPAN) & (tm < n - 1))
            def _():
                def one(t, carry):
                    v_copy(s + 1, t).wait_recv()
                    piece = stack(v_in[s, :, full(t)])
                    for c in range(0, columns, 2 * TILE):
                        cols = slice(c, c + 2 * TILE)
                        acc[:, cols] += dot3(
                            piece, (inv_h[0, full(t), cols], inv_l[0, full(t), cols])
                        )
                    return carry

                lax.fori_loop(0, tiles, one, 0)
                vec_copy(s + 1).wait_recv()
                vec_out[s] += vec_in[s + 1]

            pl.when(goes_back(s))(lambda: vec_copy(s).start())
            pad_acc[...] = jnp.zeros(pad_acc.shape, F32)
            for t in range(tiles):
                wide = slice(t * TILE, t * TILE + window)
                piece = stack(acc[:, t * TILE : (t + 1) * TILE])
                pad_acc[:, wide] += dot3t(piece, (ft_h[which, t], ft_l[which, t]))
            h, l = split(pad_acc[:, inside])
            a_hl[:rows] = h
            a_hl[rows:] = l

            def last(c, carry):
                value = w_keep[s, :, two(c)] + dot3(
                    a_hl[...], (cov_h[which, :, two(c)], cov_l[which, :, two(c)])
                )

                @pl.when(s > 0)
                def _():
                    v_out[s - 1, :, two(c)] = value
                    for i in range(2):
                        v_copy(s, 2 * c + i).start()

                @pl.when(s == 0)
                def _():
                    spread_out[:, two(c)] = value

                return carry

            lax.fori_loop(0, tiles // 2, last, 0)

        @pl.when((s == 1) & valid(SPAN))
        def _():
            for t in range(tiles // 2, tiles):
                home_copy(SPAN, t).start()

        return carry

    lax.fori_loop(0, SPAN + 1, backward, 0)
    shift_out[...] = vec_out[0, :1, :]

    @pl.when(tm < n - 1)
    def _():
        for t in range(tiles):
            home_copy(1, t).wait_recv()

    @pl.when(lends)
    def _():
        for c in lend_rows + [lend_bands, lend_means] + lend(0) + lend(1):
            c.wait_send()

    for s in range(SPAN + 1):
        if s > 0:
            pl.when(goes_back(s))(lambda s=s: vec_copy(s).wait_send())
        for t in range(tiles):
            if s < SPAN:
                pl.when(goes_on(s))(lambda s=s, t=t: x_copy(s, t).wait_send())
            if s > 0:
                pl.when(goes_home(s))(lambda s=s, t=t: home_copy(s, t).wait_send())
                pl.when(goes_back(s))(lambda s=s, t=t: v_copy(s, t).wait_send())


def body(n, n_row, covariance, precision, band_weight, band_offset, prior_mean, innovation, seen_sites):
    rows, columns = covariance.shape[1:]
    tiles = columns // TILE
    window = TILE + 2 * EDGE
    steps = SPAN + 1
    square = n_row == 4 and rows == TILE
    copies = 10 if square else n_row - 1
    slots = (7, rows, rows) if square else (n_row - 1, rows, columns)
    block = lambda *lead: pltpu.VMEM(lead + (rows, columns), F32)
    whole = pltpu.VMEM((2, columns, columns), BF16)
    vec = lambda *lead: pltpu.VMEM(lead + (VEC, rows), F32)
    padded = columns + 2 * EDGE
    dma = lambda *shape: pltpu.SemaphoreType.DMA(shape)
    vmem = pl.BlockSpec(memory_space=pltpu.VMEM)
    gain, shift, spread = pl.pallas_call(
        functools.partial(kernel, n, n_row),
        out_shape=(
            jax.ShapeDtypeStruct((rows, columns), F32),
            jax.ShapeDtypeStruct((1, rows), F32),
            jax.ShapeDtypeStruct((rows, columns), F32),
        ),
        in_specs=[pl.BlockSpec(memory_space=pltpu.SMEM)] + [vmem] * 6,
        out_specs=(vmem, vmem, vmem),
        scratch_shapes=[
            pltpu.VMEM((2, 2) + slots, F32), block(2), pltpu.VMEM((2, 16, columns), F32),
            whole, whole, whole, whole,
            pltpu.VMEM((2, tiles, window, TILE), BF16), pltpu.VMEM((2, tiles, window, TILE), BF16),
            block(SPAN), block(steps), block(steps), block(SPAN), block(SPAN),
            pltpu.VMEM((2 * rows, columns), BF16), pltpu.VMEM((2 * rows, padded), BF16),
            block(), pltpu.VMEM((rows, padded), F32),
            vec(n_row), pltpu.VMEM((2, 2, VEC, columns), F32),
            pltpu.VMEM((2, 2 * VEC, padded), BF16), pltpu.VMEM((2, 2 * VEC, columns), BF16),
            vec(steps), vec(steps), vec(steps),
            dma(2, copies), dma(2, copies), dma(2, copies), dma(2, copies), dma(4), dma(4),
            dma(n_row - 1), dma(n_row - 1),
            dma(SPAN, tiles), dma(SPAN, tiles), dma(steps, tiles), dma(tiles),
            dma(steps, tiles), dma(steps, tiles), dma(steps), dma(steps),
        ],
        compiler_params=pltpu.CompilerParams(
            collective_id=0, has_side_effects=True, vmem_limit_bytes=62 * 2**20
        ),
        cost_estimate=pl.CostEstimate(
            flops=2 * 54 * rows * columns * columns, bytes_accessed=16 * rows * columns,
            transcendentals=0,
        ),
    )(
        band_offset, covariance[0], precision[0], band_weight[0],
        prior_mean, innovation, seen_sites,
    )
    return gain[None], shift, spread[None]


def solution(mesh):
    in_specs = (
        P("tm", "row", None),
        P("tm", "row", None),
        P("tm", None, None),
        P("tm", None),
        P("tm", "row"),
        P("tm", None),
        P("tm", None),
    )
    out_specs = (P("tm", "row", None), P("tm", "row"), P("tm", "row", None))
    return jax.shard_map(
        functools.partial(body, mesh.shape["tm"], mesh.shape["row"]),
        mesh=mesh, in_specs=in_specs, out_specs=out_specs, check_vma=False,
    )
```

```python
import functools

import jax
import jax.numpy as jnp
from jax import lax
from jax.experimental import pallas as pl
from jax.experimental.pallas import tpu as pltpu
from jax.sharding import PartitionSpec as P

NBAND = 5
REACH = 64
SPAN = 3
TILE = 256
EDGE = 128
VEC = 16

MESH = pl.DeviceIdType.MESH
F32 = jnp.float32
BF16 = jnp.bfloat16


def split(value):
    high = value.astype(BF16)
    return high, (value - high.astype(F32)).astype(BF16)


def stack(value):
    return jnp.concatenate(split(value), axis=0)


def dot3(left, right):
    high, low = right
    one = functools.partial(jnp.dot, preferred_element_type=F32)
    count = left.shape[0] // 2
    both = one(left, high)
    return both[:count] + (both[count:] + one(left[:count], low))


def dot3t(left, right):
    high, low = right

    def one(a, b):
        return lax.dot_general(a, b, (((1,), (1,)), ((), ())), preferred_element_type=F32)

    count = left.shape[0] // 2
    both = one(left, high)
    return both[:count] + (both[count:] + one(left[:count], low))


def kernel(
    n, n_row,
    offsets, cov_rows, inv_rows, weights, prior, innovation, seen,
    gain_out, shift_out, spread_out,
    land, rows_two, bands, cov_h, cov_l, inv_h, inv_l, ft_h, ft_l,
    x_in, x_keep, w_keep, v_in, v_out, a_hl, pad_hl, acc, pad_acc,
    prior_all, means, f_hl, h_hl, part, vec_in, vec_out,
    g_send, g_recv, r_send, r_recv, s_send, s_recv, p_send, p_recv,
    x_send, x_recv, home_send, home_recv, v_send, v_recv, vec_send, vec_recv,
):
    tm = lax.axis_index("tm")
    row = lax.axis_index("row")
    rows, columns = cov_rows.shape
    tiles = columns // TILE
    even = lax.rem(tm, 2) == 0
    odd = lax.rem(tm, 2) == 1

    def at(index, size):
        return pl.ds(pl.multiple_of(index * size, size), size)

    def remote(src, dst, send, recv, to_tm, to_row):
        return pltpu.make_async_remote_copy(
            src_ref=src, dst_ref=dst, send_sem=send, recv_sem=recv,
            device_id=(to_tm, to_row), device_id_type=MESH,
        )

    barrier = pltpu.get_barrier_semaphore()

    def greet(t, r):
        pl.semaphore_signal(barrier, inc=1, device_id=(t, r), device_id_type=MESH)

    for d in range(1, n_row):
        greet(tm, lax.rem(row + d, n_row))
    for d in range(1, SPAN + 1):
        pl.when(tm + d < n)(lambda d=d: greet(tm + d, row))
        pl.when(tm - d >= 0)(lambda d=d: greet(tm - d, row))
    pl.semaphore_wait(
        barrier, n_row - 1 + jnp.minimum(tm, SPAN) + jnp.minimum(n - 1 - tm, SPAN)
    )

    twin = even & (tm >= 2) & (tm + 2 < n)
    lends = even & (tm >= 4)

    def valid(s):
        last = (odd & (tm >= SPAN)) | twin
        return ((s < SPAN) & (tm >= s)) | ((s == SPAN) & last)

    def goes_on(s):
        return valid(s) & (s < SPAN) & (tm + 1 < n)

    def goes_home(s):
        return valid(s) & (s > 0) & ((s == SPAN) | (tm == n - 1))

    def goes_back(s):
        return valid(s) & (s > 0)

    def chosen(s):
        return jnp.where((s == SPAN) & even, 1, 0)

    square = n_row == 4 and rows == TILE
    half = rows // 2
    if square:
        x, y = lax.rem(row, 2), row // 2
        r1, r2, r3 = 2 * y + 1 - x, 2 * (1 - y) + x, 2 * (1 - y) + 1 - x
        every, low, top = pl.ds(0, rows), pl.ds(0, half), pl.ds(half, half)
        right = pl.ds(pl.multiple_of(row * rows + half, half), half)
        right3 = pl.ds(pl.multiple_of(r3 * rows + half, half), half)
        plan = []
        for slot, to in enumerate((r1, r2, r3)):
            plan.append((to, slot, low, at(row, rows), every))
            plan.append((to, slot, top, right, top))
        plan.append((r1, 3, every, at(r2, rows), every))
        plan.append((r2, 4, every, at(r1, rows), every))
        plan.append((r1, 5, low, at(r3, rows), every))
        plan.append((r2, 6, every, right3, low))
    else:
        every = pl.ds(0, rows)
        wide = pl.ds(0, columns)
        plan = [
            (lax.rem(row + d, n_row), d - 1, every, wide, wide) for d in range(1, n_row)
        ]

    def gather(m, src):
        return [
            remote(
                src.at[rsl, csl], land.at[0, m, slot, rsl, dsl],
                g_send.at[m, c], g_recv.at[m, c], tm, to,
            )
            for c, (to, slot, rsl, csl, dsl) in enumerate(plan)
        ]

    def lend(m):
        return [
            remote(
                land.at[0, m, slot, rsl, dsl], land.at[1, m, slot, rsl, dsl],
                r_send.at[m, c], r_recv.at[m, c], tm - 2, row,
            )
            for c, (to, slot, rsl, csl, dsl) in enumerate(plan)
        ]

    def share():
        return [
            remote(
                rows_two.at[1, rsl, csl], land.at[1, 1, slot, rsl, dsl],
                r_send.at[1, c], r_recv.at[1, c], tm, to,
            )
            for c, (to, slot, rsl, csl, dsl) in enumerate(plan)
        ]

    def small(c, src, dst):
        return remote(src, dst, s_send.at[c], s_recv.at[c], tm - 2, row)

    lend_rows = [
        small(1, cov_rows, rows_two.at[1]), small(0, inv_rows, rows_two.at[0])
    ]
    lend_bands = small(2, bands.at[0], bands.at[1])
    lend_means = small(3, means.at[0], means.at[1])

    def putter(which, high, low_part):
        def put(rsl, csl, value):
            h, l = split(value)
            high[which, rsl, csl] = h
            low_part[which, rsl, csl] = l

        return put

    def fill_own(which, src, high, low_part):
        put = putter(which, high, low_part)
        put(at(row, rows), pl.ds(0, columns), src[...])
        if square:
            for r in (r1, r2, r3):
                put(at(r, rows), at(row, rows), src[:, at(r, rows)].T)

    def fill_slots(which, m, copies, high, low_part, on=None):
        put = putter(which, high, low_part)
        for slot in range(7 if square else n_row - 1):
            for c, entry in enumerate(plan):
                if entry[1] == slot:
                    copies[c].wait_recv()
                    if on is not None:
                        pl.when(lends)(lambda c=c: on[c].start())
            if not square:
                owner = lax.rem(row + n_row - 1 - slot, n_row)
                put(at(owner, rows), pl.ds(0, columns), land[which, m, slot])
            elif slot < 3:
                r = (r1, r2, r3)[slot]
                upper = pl.ds(pl.multiple_of(r * rows, half), half)
                lower = pl.ds(pl.multiple_of(r * rows + half, half), half)
                put(upper, at(r, rows), land[which, m, slot, :half, :])
                put(lower, lower, land[which, m, slot, half:, half:])
                put(lower, upper, land[which, m, slot, :half, half:].T)
            elif slot < 5:
                r = r1 if slot == 3 else r2
                block = land[which, m, slot]
                put(at(r, rows), at(r3, rows), block)
                put(at(r3, rows), at(r, rows), block.T)
            else:
                upper = pl.ds(pl.multiple_of(r1 * rows, half), half)
                lower = pl.ds(pl.multiple_of(r1 * rows + half, half), half)
                if slot == 5:
                    block = land[which, m, 5, :half, :]
                    put(upper, at(r2, rows), block)
                    put(at(r2, rows), upper, block.T)
                else:
                    block = land[which, m, 6, :, :half]
                    put(at(r2, rows), lower, block)
                    put(lower, at(r2, rows), block.T)

    inv_copies = gather(0, inv_rows)
    cov_copies = gather(1, cov_rows)
    for c in inv_copies:
        c.start()

    bands[0] = jnp.zeros(bands.shape[1:], F32)
    bands[0, :NBAND, :] = weights[...]
    for b in range(NBAND):
        bands[0, 8 + b : 9 + b, :] = jnp.full((1, columns), offsets[0, b].astype(F32))

    @pl.when(lends)
    def _():
        lend_bands.start()
        for c in lend_rows:
            c.start()

    vec_out[0] = jnp.broadcast_to(prior[...], (VEC, rows))
    prior_all[row] = vec_out[0]
    prior_copies = [
        remote(
            vec_out.at[0], prior_all.at[row], p_send.at[d - 1], p_recv.at[d - 1],
            tm, lax.rem(row + d, n_row),
        )
        for d in range(1, n_row)
    ]
    for c in prior_copies:
        c.start()

    window = TILE + 2 * EDGE

    def windows(which):
        apart = lax.broadcasted_iota(jnp.int32, (window, TILE), 0) - (
            lax.broadcasted_iota(jnp.int32, (window, TILE), 1) + EDGE
        )
        apart = apart.astype(F32)
        for t in range(tiles):
            cols = slice(t * TILE, (t + 1) * TILE)
            total = jnp.zeros((window, TILE), F32)
            for b in range(NBAND):
                hit = apart == bands[which, 8 + b : 9 + b, cols]
                total = total + jnp.where(hit, bands[which, b : b + 1, cols], 0.0)
            h, l = split(total)
            ft_h[which, t] = h
            ft_l[which, t] = l

    windows(0)

    zeros = jnp.zeros((rows, EDGE), BF16)
    for first in (0, rows):
        pad_hl[first : first + rows, :EDGE] = zeros
        pad_hl[first : first + rows, EDGE + columns :] = zeros

    def full(t):
        return pl.ds(pl.multiple_of(t * TILE, TILE), TILE)

    def x_copy(s, t):
        to = jnp.where((s == SPAN - 1) & odd, tm - 1, tm + 1)
        return remote(
            x_keep.at[s, :, full(t)], x_in.at[s, :, full(t)],
            x_send.at[s, t], x_recv.at[s, t], to, row,
        )

    def home_copy(s, t):
        to = tm - jnp.where((s == SPAN) & even, 1, s)
        return remote(
            x_keep.at[s, :, full(t)], gain_out.at[:, full(t)],
            home_send.at[s, t], home_recv.at[t], to, row,
        )

    def back_to(s):
        return jnp.where((s == SPAN) & even, tm + 1, tm - 1)

    def v_copy(s, t):
        return remote(
            v_out.at[s - 1, :, full(t)], v_in.at[s - 1, :, full(t)],
            v_send.at[s, t], v_recv.at[s, t], back_to(s), row,
        )

    def vec_copy(s):
        return remote(
            vec_out.at[s], vec_in.at[s], vec_send.at[s], vec_recv.at[s], back_to(s), row
        )

    pair = 2 * TILE

    def two(c):
        return pl.ds(pl.multiple_of(c * pair, pair), pair)

    def band_step(s, which):
        h, l = split(w_keep[s])
        pad_hl[:rows, EDGE : EDGE + columns] = h
        pad_hl[rows:, EDGE : EDGE + columns] = l
        for t in range(tiles):
            wide = slice(t * TILE, t * TILE + window)
            cols = slice(t * TILE, (t + 1) * TILE)
            h, l = split(dot3(pad_hl[:, wide], (ft_h[which, t], ft_l[which, t])))
            a_hl[:rows, cols] = h
            a_hl[rows:, cols] = l

    def gain_step(s, which):
        def one(c, carry):
            x_keep[s, :, two(c)] = dot3(
                a_hl[...], (inv_h[which, :, two(c)], inv_l[which, :, two(c)])
            )
            for i in range(2):
                t = 2 * c + i
                pl.when(goes_on(s))(lambda t=t: x_copy(s, t).start())
                early = goes_home(s) & ((s < SPAN) | (t < tiles // 2))
                pl.when(early)(lambda t=t: home_copy(s, t).start())
            return carry

        lax.fori_loop(0, tiles // 2, one, 0)

    w_keep[0] = cov_rows[...]
    band_step(0, 0)
    fill_own(0, inv_rows, inv_h, inv_l)
    fill_own(0, cov_rows, cov_h, cov_l)
    ahead = len(plan) - 4 if square else len(plan)
    for c in inv_copies[:ahead]:
        c.wait_send()
    for c in cov_copies:
        c.start()
    fill_slots(0, 0, inv_copies, inv_h, inv_l, lend(0))
    gain_step(0, 0)

    @pl.when(tm == n - 1)
    def _():
        gain_out[...] = x_keep[0]

    count = seen.shape[1]
    spots = jnp.broadcast_to(seen[...].astype(F32), (count, count)).T
    lanes = lax.broadcasted_iota(jnp.int32, (count, count), 1).astype(F32)
    matches = jnp.concatenate(
        [
            jnp.where(lanes + float(c * count) == spots, 1.0, 0.0)
            for c in range(columns // count)
        ],
        axis=1,
    ).astype(BF16)
    values = jnp.broadcast_to(innovation[...], (VEC, count))
    first, second = split(values)
    third = (values - first.astype(F32) - second.astype(F32)).astype(BF16)
    total = jnp.zeros((VEC, columns), F32)
    for piece in (third, second, first):
        total = total + jnp.dot(piece, matches, preferred_element_type=F32)
    pulled = stack(total)
    own = vec_out[0] + dot3t(pulled, split(cov_rows[...]))
    for c in prior_copies:
        c.wait()
    for c in inv_copies[ahead:] + cov_copies:
        c.wait_send()

    @pl.when(twin)
    def _():
        lend_rows[0].wait_recv()
        for c in share():
            c.start()

    fill_slots(0, 1, cov_copies, cov_h, cov_l)
    inside = slice(EDGE, EDGE + columns)

    def cut_means(which):
        zeros = jnp.zeros((2 * VEC, EDGE), BF16)
        f_hl[which, :, :EDGE] = zeros
        f_hl[which, :, EDGE + columns :] = zeros
        f_hl[which, :, inside] = stack(means[which, 0])

    def cut_moved(which):
        h_hl[which] = stack(means[which, 1])

    def filtered():
        prior_row = jnp.concatenate([prior_all[r] for r in range(n_row)], axis=1)
        for t in range(tiles):
            cols = slice(t * TILE, (t + 1) * TILE)
            means[0, 0, :, cols] = prior_row[:, cols] + dot3(
                pulled, (cov_h[0, :, cols], cov_l[0, :, cols])
            )
        cut_means(0)
        for t in range(tiles):
            wide = slice(t * TILE, t * TILE + window)
            means[0, 1, :, t * TILE : (t + 1) * TILE] = dot3(
                f_hl[0, :, wide], (ft_h[0, t], ft_l[0, t])
            )
        cut_moved(0)
        pl.when(lends)(lambda: lend_means.start())

    def moved_part(s, which):
        return dot3t(h_hl[which], split(x_keep[s]))

    def forward(s, carry):
        which = chosen(s)

        @pl.when(twin & (s == SPAN))
        def _():
            lend_means.wait_recv()
            cut_means(1)
            cut_moved(1)

        @pl.when(valid(s))
        def _():
            w_keep[s] = jnp.zeros((rows, columns), F32)

            def one(t, carry):
                x_copy(s - 1, t).wait_recv()
                piece = stack(x_in[s - 1, :, full(t)])
                for c in range(0, columns, 2 * TILE):
                    cols = slice(c, c + 2 * TILE)
                    w_keep[s, :, cols] += dot3(
                        piece, (cov_h[which, full(t), cols], cov_l[which, full(t), cols])
                    )
                return carry

            lax.fori_loop(0, tiles, one, 0)
            band_step(s, which)
            gain_step(s, which)

        @pl.when(s == 1)
        def _():
            filtered()
            part[0] = own - moved_part(0, 0)

        @pl.when(valid(s))
        def _():
            part[s] = dot3t(f_hl[which, :, inside], split(x_in[s - 1])) - moved_part(s, which)

        @pl.when(twin & (s == 1))
        def _():
            lend_bands.wait_recv()
            windows(1)
            lend_rows[1].wait_recv()
            fill_own(1, rows_two.at[0], inv_h, inv_l)
            fill_slots(1, 0, lend(0), inv_h, inv_l)
            fill_own(1, rows_two.at[1], cov_h, cov_l)
            fill_slots(1, 1, share(), cov_h, cov_l)

        return carry

    lax.fori_loop(1, SPAN + 1, forward, 0)

    def backward(i, carry):
        s = SPAN - i
        which = chosen(s)

        @pl.when(valid(s))
        def _():
            acc[...] = -x_keep[s]
            vec_out[s] = part[s]

            @pl.when((s < SPAN) & (tm < n - 1))
            def _():
                def one(t, carry):
                    v_copy(s + 1, t).wait_recv()
                    piece = stack(v_in[s, :, full(t)])
                    for c in range(0, columns, 2 * TILE):
                        cols = slice(c, c + 2 * TILE)
                        acc[:, cols] += dot3(
                            piece, (inv_h[0, full(t), cols], inv_l[0, full(t), cols])
                        )
                    return carry

                lax.fori_loop(0, tiles, one, 0)
                vec_copy(s + 1).wait_recv()
                vec_out[s] += vec_in[s + 1]

            pl.when(goes_back(s))(lambda: vec_copy(s).start())
            pad_acc[...] = jnp.zeros(pad_acc.shape, F32)
            for t in range(tiles):
                wide = slice(t * TILE, t * TILE + window)
                piece = stack(acc[:, t * TILE : (t + 1) * TILE])
                pad_acc[:, wide] += dot3t(piece, (ft_h[which, t], ft_l[which, t]))
            h, l = split(pad_acc[:, inside])
            a_hl[:rows] = h
            a_hl[rows:] = l

            def last(c, carry):
                value = w_keep[s, :, two(c)] + dot3(
                    a_hl[...], (cov_h[which, :, two(c)], cov_l[which, :, two(c)])
                )

                @pl.when(s > 0)
                def _():
                    v_out[s - 1, :, two(c)] = value
                    for i in range(2):
                        v_copy(s, 2 * c + i).start()

                @pl.when(s == 0)
                def _():
                    spread_out[:, two(c)] = value

                return carry

            lax.fori_loop(0, tiles // 2, last, 0)

        @pl.when((s == 1) & valid(SPAN))
        def _():
            for t in range(tiles // 2, tiles):
                home_copy(SPAN, t).start()

        return carry

    lax.fori_loop(0, SPAN + 1, backward, 0)
    shift_out[...] = vec_out[0, :1, :]

    @pl.when(tm < n - 1)
    def _():
        for t in range(tiles):
            home_copy(1, t).wait_recv()

    @pl.when(lends)
    def _():
        for c in lend_rows + [lend_bands, lend_means] + lend(0):
            c.wait_send()

    @pl.when(twin)
    def _():
        for c in share():
            c.wait_send()

    for s in range(SPAN + 1):
        if s > 0:
            pl.when(goes_back(s))(lambda s=s: vec_copy(s).wait_send())
        for t in range(tiles):
            if s < SPAN:
                pl.when(goes_on(s))(lambda s=s, t=t: x_copy(s, t).wait_send())
            if s > 0:
                pl.when(goes_home(s))(lambda s=s, t=t: home_copy(s, t).wait_send())
                pl.when(goes_back(s))(lambda s=s, t=t: v_copy(s, t).wait_send())


def body(n, n_row, covariance, precision, band_weight, band_offset, prior_mean, innovation, seen_sites):
    rows, columns = covariance.shape[1:]
    tiles = columns // TILE
    window = TILE + 2 * EDGE
    steps = SPAN + 1
    square = n_row == 4 and rows == TILE
    copies = 10 if square else n_row - 1
    slots = (7, rows, rows) if square else (n_row - 1, rows, columns)
    block = lambda *lead: pltpu.VMEM(lead + (rows, columns), F32)
    whole = pltpu.VMEM((2, columns, columns), BF16)
    vec = lambda *lead: pltpu.VMEM(lead + (VEC, rows), F32)
    padded = columns + 2 * EDGE
    dma = lambda *shape: pltpu.SemaphoreType.DMA(shape)
    vmem = pl.BlockSpec(memory_space=pltpu.VMEM)
    gain, shift, spread = pl.pallas_call(
        functools.partial(kernel, n, n_row),
        out_shape=(
            jax.ShapeDtypeStruct((rows, columns), F32),
            jax.ShapeDtypeStruct((1, rows), F32),
            jax.ShapeDtypeStruct((rows, columns), F32),
        ),
        in_specs=[pl.BlockSpec(memory_space=pltpu.SMEM)] + [vmem] * 6,
        out_specs=(vmem, vmem, vmem),
        scratch_shapes=[
            pltpu.VMEM((2, 2) + slots, F32), block(2), pltpu.VMEM((2, 16, columns), F32),
            whole, whole, whole, whole,
            pltpu.VMEM((2, tiles, window, TILE), BF16), pltpu.VMEM((2, tiles, window, TILE), BF16),
            block(SPAN), block(steps), block(steps), block(SPAN), block(SPAN),
            pltpu.VMEM((2 * rows, columns), BF16), pltpu.VMEM((2 * rows, padded), BF16),
            block(), pltpu.VMEM((rows, padded), F32),
            vec(n_row), pltpu.VMEM((2, 2, VEC, columns), F32),
            pltpu.VMEM((2, 2 * VEC, padded), BF16), pltpu.VMEM((2, 2 * VEC, columns), BF16),
            vec(steps), vec(steps), vec(steps),
            dma(2, copies), dma(2, copies), dma(2, copies), dma(2, copies), dma(4), dma(4),
            dma(n_row - 1), dma(n_row - 1),
            dma(SPAN, tiles), dma(SPAN, tiles), dma(steps, tiles), dma(tiles),
            dma(steps, tiles), dma(steps, tiles), dma(steps), dma(steps),
        ],
        compiler_params=pltpu.CompilerParams(
            collective_id=0, has_side_effects=True, vmem_limit_bytes=62 * 2**20
        ),
        cost_estimate=pl.CostEstimate(
            flops=2 * 54 * rows * columns * columns, bytes_accessed=16 * rows * columns,
            transcendentals=0,
        ),
    )(
        band_offset, covariance[0], precision[0], band_weight[0],
        prior_mean, innovation, seen_sites,
    )
    return gain[None], shift, spread[None]


def solution(mesh):
    in_specs = (
        P("tm", "row", None),
        P("tm", "row", None),
        P("tm", None, None),
        P("tm", None),
        P("tm", "row"),
        P("tm", None),
        P("tm", None),
    )
    out_specs = (P("tm", "row", None), P("tm", "row"), P("tm", "row", None))
    return jax.shard_map(
        functools.partial(body, mesh.shape["tm"], mesh.shape["row"]),
        mesh=mesh, in_specs=in_specs, out_specs=out_specs, check_vma=False,
    )
```

```python
import functools

import jax
import jax.numpy as jnp
from jax import lax
from jax.experimental import pallas as pl
from jax.experimental.pallas import tpu as pltpu
from jax.sharding import PartitionSpec as P

NBAND = 5
REACH = 64
SPAN = 3
TILE = 256
EDGE = 128
VEC = 16

MESH = pl.DeviceIdType.MESH
F32 = jnp.float32
BF16 = jnp.bfloat16


def split(value):
    high = value.astype(BF16)
    return high, (value - high.astype(F32)).astype(BF16)


def stack(value):
    return jnp.concatenate(split(value), axis=0)


def dot3(left, right):
    high, low = right
    one = functools.partial(jnp.dot, preferred_element_type=F32)
    count = left.shape[0] // 2
    both = one(left, high)
    return both[:count] + (both[count:] + one(left[:count], low))


def dot3t(left, right):
    high, low = right

    def one(a, b):
        return lax.dot_general(a, b, (((1,), (1,)), ((), ())), preferred_element_type=F32)

    count = left.shape[0] // 2
    both = one(left, high)
    return both[:count] + (both[count:] + one(left[:count], low))


def kernel(
    n, n_row,
    offsets, cov_rows, inv_rows, weights, prior, innovation, seen,
    gain_out, shift_out, spread_out,
    land, rows_two, bands, cov_h, cov_l, inv_h, inv_l, ft_h, ft_l,
    x_in, x_keep, w_keep, v_in, v_out, a_hl, pad_hl, acc, pad_acc,
    prior_all, means, f_hl, h_hl, part, vec_in, vec_out,
    g_send, g_recv, r_send, r_recv, s_send, s_recv, p_send, p_recv,
    x_send, x_recv, home_send, home_recv, v_send, v_recv, vec_send, vec_recv,
):
    tm = lax.axis_index("tm")
    row = lax.axis_index("row")
    rows, columns = cov_rows.shape
    tiles = columns // TILE
    even = lax.rem(tm, 2) == 0
    odd = lax.rem(tm, 2) == 1

    def at(index, size):
        return pl.ds(pl.multiple_of(index * size, size), size)

    def remote(src, dst, send, recv, to_tm, to_row):
        return pltpu.make_async_remote_copy(
            src_ref=src, dst_ref=dst, send_sem=send, recv_sem=recv,
            device_id=(to_tm, to_row), device_id_type=MESH,
        )

    barrier = pltpu.get_barrier_semaphore()

    def greet(t, r):
        pl.semaphore_signal(barrier, inc=1, device_id=(t, r), device_id_type=MESH)

    for d in range(1, n_row):
        greet(tm, lax.rem(row + d, n_row))
    for d in range(1, SPAN + 1):
        pl.when(tm + d < n)(lambda d=d: greet(tm + d, row))
        pl.when(tm - d >= 0)(lambda d=d: greet(tm - d, row))
    pl.semaphore_wait(
        barrier, n_row - 1 + jnp.minimum(tm, SPAN) + jnp.minimum(n - 1 - tm, SPAN)
    )

    twin = even & (tm >= 2) & (tm + 2 < n)
    lends = even & (tm >= 4)

    def valid(s):
        last = (odd & (tm >= SPAN)) | twin
        return ((s < SPAN) & (tm >= s)) | ((s == SPAN) & last)

    def goes_on(s):
        return valid(s) & (s < SPAN) & (tm + 1 < n)

    def goes_home(s):
        return valid(s) & (s > 0) & ((s == SPAN) | (tm == n - 1))

    def goes_back(s):
        return valid(s) & (s > 0)

    def chosen(s):
        return jnp.where((s == SPAN) & even, 1, 0)

    square = n_row == 4 and rows == TILE
    half = rows // 2
    if square:
        x, y = lax.rem(row, 2), row // 2
        r1, r2, r3 = 2 * y + 1 - x, 2 * (1 - y) + x, 2 * (1 - y) + 1 - x
        every, low, top = pl.ds(0, rows), pl.ds(0, half), pl.ds(half, half)
        right = pl.ds(pl.multiple_of(row * rows + half, half), half)
        right3 = pl.ds(pl.multiple_of(r3 * rows + half, half), half)
        plan = []
        for slot, to in enumerate((r1, r2, r3)):
            plan.append((to, slot, low, at(row, rows), every))
            plan.append((to, slot, top, right, top))
        plan.append((r1, 3, every, at(r2, rows), every))
        plan.append((r2, 4, every, at(r1, rows), every))
        plan.append((r1, 5, low, at(r3, rows), every))
        plan.append((r2, 6, every, right3, low))
    else:
        every = pl.ds(0, rows)
        wide = pl.ds(0, columns)
        plan = [
            (lax.rem(row + d, n_row), d - 1, every, wide, wide) for d in range(1, n_row)
        ]

    def gather(m, src):
        return [
            remote(
                src.at[rsl, csl], land.at[0, m, slot, rsl, dsl],
                g_send.at[m, c], g_recv.at[m, c], tm, to,
            )
            for c, (to, slot, rsl, csl, dsl) in enumerate(plan)
        ]

    def lend(m):
        return [
            remote(
                land.at[0, m, slot, rsl, dsl], land.at[1, m, slot, rsl, dsl],
                r_send.at[m, c], r_recv.at[m, c], tm - 2, row,
            )
            for c, (to, slot, rsl, csl, dsl) in enumerate(plan)
        ]

    def share():
        return [
            remote(
                rows_two.at[1, rsl, csl], land.at[1, 1, slot, rsl, dsl],
                r_send.at[1, c], r_recv.at[1, c], tm, to,
            )
            for c, (to, slot, rsl, csl, dsl) in enumerate(plan)
        ]

    def small(c, src, dst):
        return remote(src, dst, s_send.at[c], s_recv.at[c], tm - 2, row)

    lend_rows = [
        small(1, cov_rows, rows_two.at[1]), small(0, inv_rows, rows_two.at[0])
    ]
    lend_bands = small(2, bands.at[0], bands.at[1])
    lend_means = small(3, means.at[0], means.at[1])

    def putter(which, high, low_part):
        def put(rsl, csl, value):
            h, l = split(value)
            high[which, rsl, csl] = h
            low_part[which, rsl, csl] = l

        return put

    def fill_own(which, src, high, low_part):
        put = putter(which, high, low_part)
        put(at(row, rows), pl.ds(0, columns), src[...])
        if square:
            for r in (r1, r2, r3):
                put(at(r, rows), at(row, rows), src[:, at(r, rows)].T)

    def fill_slots(which, m, copies, high, low_part, on=None):
        put = putter(which, high, low_part)
        for slot in range(7 if square else n_row - 1):
            for c, entry in enumerate(plan):
                if entry[1] == slot:
                    copies[c].wait_recv()
                    if on is not None:
                        pl.when(lends)(lambda c=c: on[c].start())
            if not square:
                owner = lax.rem(row + n_row - 1 - slot, n_row)
                put(at(owner, rows), pl.ds(0, columns), land[which, m, slot])
            elif slot < 3:
                r = (r1, r2, r3)[slot]
                upper = pl.ds(pl.multiple_of(r * rows, half), half)
                lower = pl.ds(pl.multiple_of(r * rows + half, half), half)
                put(upper, at(r, rows), land[which, m, slot, :half, :])
                put(lower, lower, land[which, m, slot, half:, half:])
                put(lower, upper, land[which, m, slot, :half, half:].T)
            elif slot < 5:
                r = r1 if slot == 3 else r2
                block = land[which, m, slot]
                put(at(r, rows), at(r3, rows), block)
                put(at(r3, rows), at(r, rows), block.T)
            else:
                upper = pl.ds(pl.multiple_of(r1 * rows, half), half)
                lower = pl.ds(pl.multiple_of(r1 * rows + half, half), half)
                if slot == 5:
                    block = land[which, m, 5, :half, :]
                    put(upper, at(r2, rows), block)
                    put(at(r2, rows), upper, block.T)
                else:
                    block = land[which, m, 6, :, :half]
                    put(at(r2, rows), lower, block)
                    put(lower, at(r2, rows), block.T)

    inv_copies = gather(0, inv_rows)
    cov_copies = gather(1, cov_rows)
    for c in inv_copies:
        c.start()

    bands[0] = jnp.zeros(bands.shape[1:], F32)
    bands[0, :NBAND, :] = weights[...]
    for b in range(NBAND):
        bands[0, 8 + b : 9 + b, :] = jnp.full((1, columns), offsets[0, b].astype(F32))

    @pl.when(lends)
    def _():
        lend_bands.start()
        for c in lend_rows:
            c.start()

    vec_out[0] = jnp.broadcast_to(prior[...], (VEC, rows))
    prior_all[row] = vec_out[0]
    prior_copies = [
        remote(
            vec_out.at[0], prior_all.at[row], p_send.at[d - 1], p_recv.at[d - 1],
            tm, lax.rem(row + d, n_row),
        )
        for d in range(1, n_row)
    ]
    for c in prior_copies:
        c.start()

    window = TILE + 2 * EDGE

    def windows(which):
        apart = lax.broadcasted_iota(jnp.int32, (window, TILE), 0) - (
            lax.broadcasted_iota(jnp.int32, (window, TILE), 1) + EDGE
        )
        apart = apart.astype(F32)
        for t in range(tiles):
            cols = slice(t * TILE, (t + 1) * TILE)
            total = jnp.zeros((window, TILE), F32)
            for b in range(NBAND):
                hit = apart == bands[which, 8 + b : 9 + b, cols]
                total = total + jnp.where(hit, bands[which, b : b + 1, cols], 0.0)
            h, l = split(total)
            ft_h[which, t] = h
            ft_l[which, t] = l

    windows(0)

    zeros = jnp.zeros((rows, EDGE), BF16)
    for first in (0, rows):
        pad_hl[first : first + rows, :EDGE] = zeros
        pad_hl[first : first + rows, EDGE + columns :] = zeros

    def full(t):
        return pl.ds(pl.multiple_of(t * TILE, TILE), TILE)

    def x_copy(s, t):
        to = jnp.where((s == SPAN - 1) & odd, tm - 1, tm + 1)
        return remote(
            x_keep.at[s, :, full(t)], x_in.at[s, :, full(t)],
            x_send.at[s, t], x_recv.at[s, t], to, row,
        )

    def home_copy(s, t):
        to = tm - jnp.where((s == SPAN) & even, 1, s)
        return remote(
            x_keep.at[s, :, full(t)], gain_out.at[:, full(t)],
            home_send.at[s, t], home_recv.at[t], to, row,
        )

    def back_to(s):
        return jnp.where((s == SPAN) & even, tm + 1, tm - 1)

    def v_copy(s, t):
        return remote(
            v_out.at[s - 1, :, full(t)], v_in.at[s - 1, :, full(t)],
            v_send.at[s, t], v_recv.at[s, t], back_to(s), row,
        )

    def vec_copy(s):
        return remote(
            vec_out.at[s], vec_in.at[s], vec_send.at[s], vec_recv.at[s], back_to(s), row
        )

    pair = 2 * TILE

    def two(c):
        return pl.ds(pl.multiple_of(c * pair, pair), pair)

    def band_step(s, which):
        h, l = split(w_keep[s])
        pad_hl[:rows, EDGE : EDGE + columns] = h
        pad_hl[rows:, EDGE : EDGE + columns] = l
        for t in range(tiles):
            wide = slice(t * TILE, t * TILE + window)
            cols = slice(t * TILE, (t + 1) * TILE)
            h, l = split(dot3(pad_hl[:, wide], (ft_h[which, t], ft_l[which, t])))
            a_hl[:rows, cols] = h
            a_hl[rows:, cols] = l

    def gain_step(s, which):
        def one(c, carry):
            x_keep[s, :, two(c)] = dot3(
                a_hl[...], (inv_h[which, :, two(c)], inv_l[which, :, two(c)])
            )
            for i in range(2):
                t = 2 * c + i
                pl.when(goes_on(s))(lambda t=t: x_copy(s, t).start())
                early = goes_home(s) & ((s < SPAN) | (t < tiles // 2))
                pl.when(early)(lambda t=t: home_copy(s, t).start())
            return carry

        lax.fori_loop(0, tiles // 2, one, 0)

    w_keep[0] = cov_rows[...]
    band_step(0, 0)
    fill_own(0, inv_rows, inv_h, inv_l)
    fill_own(0, cov_rows, cov_h, cov_l)
    ahead = len(plan) - 4 if square else len(plan)
    for c in inv_copies[:ahead]:
        c.wait_send()
    for c in cov_copies:
        c.start()
    fill_slots(0, 0, inv_copies, inv_h, inv_l, lend(0))
    gain_step(0, 0)

    @pl.when(tm == n - 1)
    def _():
        gain_out[...] = x_keep[0]

    count = seen.shape[1]
    spots = jnp.broadcast_to(seen[...].astype(F32), (count, count)).T
    lanes = lax.broadcasted_iota(jnp.int32, (count, count), 1).astype(F32)
    matches = jnp.concatenate(
        [
            jnp.where(lanes + float(c * count) == spots, 1.0, 0.0)
            for c in range(columns // count)
        ],
        axis=1,
    ).astype(BF16)
    values = jnp.broadcast_to(innovation[...], (VEC, count))
    first, second = split(values)
    third = (values - first.astype(F32) - second.astype(F32)).astype(BF16)
    total = jnp.zeros((VEC, columns), F32)
    for piece in (third, second, first):
        total = total + jnp.dot(piece, matches, preferred_element_type=F32)
    pulled = stack(total)
    own = vec_out[0] + dot3t(pulled, split(cov_rows[...]))
    for c in prior_copies:
        c.wait()
    @pl.when(twin)
    def _():
        lend_bands.wait_recv()
        windows(1)
        for c in lend_rows:
            c.wait_recv()
        fill_own(1, rows_two.at[1], cov_h, cov_l)
        fill_own(1, rows_two.at[0], inv_h, inv_l)

    for c in inv_copies[ahead:] + cov_copies:
        c.wait_send()

    @pl.when(twin)
    def _():
        for c in share():
            c.start()

    fill_slots(0, 1, cov_copies, cov_h, cov_l)
    inside = slice(EDGE, EDGE + columns)

    def cut_means(which):
        zeros = jnp.zeros((2 * VEC, EDGE), BF16)
        f_hl[which, :, :EDGE] = zeros
        f_hl[which, :, EDGE + columns :] = zeros
        f_hl[which, :, inside] = stack(means[which, 0])

    def cut_moved(which):
        h_hl[which] = stack(means[which, 1])

    def filtered():
        prior_row = jnp.concatenate([prior_all[r] for r in range(n_row)], axis=1)
        for t in range(tiles):
            cols = slice(t * TILE, (t + 1) * TILE)
            means[0, 0, :, cols] = prior_row[:, cols] + dot3(
                pulled, (cov_h[0, :, cols], cov_l[0, :, cols])
            )
        cut_means(0)
        for t in range(tiles):
            wide = slice(t * TILE, t * TILE + window)
            means[0, 1, :, t * TILE : (t + 1) * TILE] = dot3(
                f_hl[0, :, wide], (ft_h[0, t], ft_l[0, t])
            )
        cut_moved(0)
        pl.when(lends)(lambda: lend_means.start())

    def moved_part(s, which):
        return dot3t(h_hl[which], split(x_keep[s]))

    def forward(s, carry):
        which = chosen(s)

        @pl.when(twin & (s == SPAN))
        def _():
            lend_means.wait_recv()
            cut_means(1)
            cut_moved(1)

        @pl.when(valid(s))
        def _():
            w_keep[s] = jnp.zeros((rows, columns), F32)

            def one(t, carry):
                x_copy(s - 1, t).wait_recv()
                piece = stack(x_in[s - 1, :, full(t)])
                for c in range(0, columns, 2 * TILE):
                    cols = slice(c, c + 2 * TILE)
                    w_keep[s, :, cols] += dot3(
                        piece, (cov_h[which, full(t), cols], cov_l[which, full(t), cols])
                    )
                return carry

            lax.fori_loop(0, tiles, one, 0)
            band_step(s, which)
            gain_step(s, which)

        @pl.when(s == 1)
        def _():
            filtered()
            part[0] = own - moved_part(0, 0)

        @pl.when(valid(s))
        def _():
            part[s] = dot3t(f_hl[which, :, inside], split(x_in[s - 1])) - moved_part(s, which)

        @pl.when(twin & (s == 1))
        def _():
            fill_slots(1, 0, lend(0), inv_h, inv_l)
            fill_slots(1, 1, share(), cov_h, cov_l)

        return carry

    lax.fori_loop(1, SPAN + 1, forward, 0)

    def backward(i, carry):
        s = SPAN - i
        which = chosen(s)

        @pl.when(valid(s))
        def _():
            acc[...] = -x_keep[s]
            vec_out[s] = part[s]

            @pl.when((s < SPAN) & (tm < n - 1))
            def _():
                def one(t, carry):
                    v_copy(s + 1, t).wait_recv()
                    piece = stack(v_in[s, :, full(t)])
                    for c in range(0, columns, 2 * TILE):
                        cols = slice(c, c + 2 * TILE)
                        acc[:, cols] += dot3(
                            piece, (inv_h[0, full(t), cols], inv_l[0, full(t), cols])
                        )
                    return carry

                lax.fori_loop(0, tiles, one, 0)
                vec_copy(s + 1).wait_recv()
                vec_out[s] += vec_in[s + 1]

            pl.when(goes_back(s))(lambda: vec_copy(s).start())
            pad_acc[...] = jnp.zeros(pad_acc.shape, F32)
            for t in range(tiles):
                wide = slice(t * TILE, t * TILE + window)
                piece = stack(acc[:, t * TILE : (t + 1) * TILE])
                pad_acc[:, wide] += dot3t(piece, (ft_h[which, t], ft_l[which, t]))
            h, l = split(pad_acc[:, inside])
            a_hl[:rows] = h
            a_hl[rows:] = l

            def last(c, carry):
                value = w_keep[s, :, two(c)] + dot3(
                    a_hl[...], (cov_h[which, :, two(c)], cov_l[which, :, two(c)])
                )

                @pl.when(s > 0)
                def _():
                    v_out[s - 1, :, two(c)] = value
                    for i in range(2):
                        v_copy(s, 2 * c + i).start()

                @pl.when(s == 0)
                def _():
                    spread_out[:, two(c)] = value

                return carry

            lax.fori_loop(0, tiles // 2, last, 0)

        @pl.when((s == 1) & valid(SPAN))
        def _():
            for t in range(tiles // 2, tiles):
                home_copy(SPAN, t).start()

        return carry

    lax.fori_loop(0, SPAN + 1, backward, 0)
    shift_out[...] = vec_out[0, :1, :]

    @pl.when(tm < n - 1)
    def _():
        for t in range(tiles):
            home_copy(1, t).wait_recv()

    @pl.when(lends)
    def _():
        for c in lend_rows + [lend_bands, lend_means] + lend(0):
            c.wait_send()

    @pl.when(twin)
    def _():
        for c in share():
            c.wait_send()

    for s in range(SPAN + 1):
        if s > 0:
            pl.when(goes_back(s))(lambda s=s: vec_copy(s).wait_send())
        for t in range(tiles):
            if s < SPAN:
                pl.when(goes_on(s))(lambda s=s, t=t: x_copy(s, t).wait_send())
            if s > 0:
                pl.when(goes_home(s))(lambda s=s, t=t: home_copy(s, t).wait_send())
                pl.when(goes_back(s))(lambda s=s, t=t: v_copy(s, t).wait_send())


def body(n, n_row, covariance, precision, band_weight, band_offset, prior_mean, innovation, seen_sites):
    rows, columns = covariance.shape[1:]
    tiles = columns // TILE
    window = TILE + 2 * EDGE
    steps = SPAN + 1
    square = n_row == 4 and rows == TILE
    copies = 10 if square else n_row - 1
    slots = (7, rows, rows) if square else (n_row - 1, rows, columns)
    block = lambda *lead: pltpu.VMEM(lead + (rows, columns), F32)
    whole = pltpu.VMEM((2, columns, columns), BF16)
    vec = lambda *lead: pltpu.VMEM(lead + (VEC, rows), F32)
    padded = columns + 2 * EDGE
    dma = lambda *shape: pltpu.SemaphoreType.DMA(shape)
    vmem = pl.BlockSpec(memory_space=pltpu.VMEM)
    gain, shift, spread = pl.pallas_call(
        functools.partial(kernel, n, n_row),
        out_shape=(
            jax.ShapeDtypeStruct((rows, columns), F32),
            jax.ShapeDtypeStruct((1, rows), F32),
            jax.ShapeDtypeStruct((rows, columns), F32),
        ),
        in_specs=[pl.BlockSpec(memory_space=pltpu.SMEM)] + [vmem] * 6,
        out_specs=(vmem, vmem, vmem),
        scratch_shapes=[
            pltpu.VMEM((2, 2) + slots, F32), block(2), pltpu.VMEM((2, 16, columns), F32),
            whole, whole, whole, whole,
            pltpu.VMEM((2, tiles, window, TILE), BF16), pltpu.VMEM((2, tiles, window, TILE), BF16),
            block(SPAN), block(steps), block(steps), block(SPAN), block(SPAN),
            pltpu.VMEM((2 * rows, columns), BF16), pltpu.VMEM((2 * rows, padded), BF16),
            block(), pltpu.VMEM((rows, padded), F32),
            vec(n_row), pltpu.VMEM((2, 2, VEC, columns), F32),
            pltpu.VMEM((2, 2 * VEC, padded), BF16), pltpu.VMEM((2, 2 * VEC, columns), BF16),
            vec(steps), vec(steps), vec(steps),
            dma(2, copies), dma(2, copies), dma(2, copies), dma(2, copies), dma(4), dma(4),
            dma(n_row - 1), dma(n_row - 1),
            dma(SPAN, tiles), dma(SPAN, tiles), dma(steps, tiles), dma(tiles),
            dma(steps, tiles), dma(steps, tiles), dma(steps), dma(steps),
        ],
        compiler_params=pltpu.CompilerParams(
            collective_id=0, has_side_effects=True, vmem_limit_bytes=62 * 2**20
        ),
        cost_estimate=pl.CostEstimate(
            flops=2 * 54 * rows * columns * columns, bytes_accessed=16 * rows * columns,
            transcendentals=0,
        ),
    )(
        band_offset, covariance[0], precision[0], band_weight[0],
        prior_mean, innovation, seen_sites,
    )
    return gain[None], shift, spread[None]


def solution(mesh):
    in_specs = (
        P("tm", "row", None),
        P("tm", "row", None),
        P("tm", None, None),
        P("tm", None),
        P("tm", "row"),
        P("tm", None),
        P("tm", None),
    )
    out_specs = (P("tm", "row", None), P("tm", "row"), P("tm", "row", None))
    return jax.shard_map(
        functools.partial(body, mesh.shape["tm"], mesh.shape["row"]),
        mesh=mesh, in_specs=in_specs, out_specs=out_specs, check_vma=False,
    )
```

```python
import functools

import jax
import jax.numpy as jnp
from jax import lax
from jax.experimental import pallas as pl
from jax.experimental.pallas import tpu as pltpu
from jax.sharding import PartitionSpec as P

NBAND = 5
REACH = 64
SPAN = 3
TILE = 256
EDGE = 128
VEC = 16

MESH = pl.DeviceIdType.MESH
F32 = jnp.float32
BF16 = jnp.bfloat16


def split(value):
    high = value.astype(BF16)
    return high, (value - high.astype(F32)).astype(BF16)


def stack(value):
    return jnp.concatenate(split(value), axis=0)


def dot3(left, right):
    high, low = right
    one = functools.partial(jnp.dot, preferred_element_type=F32)
    count = left.shape[0] // 2
    both = one(left, high)
    return both[:count] + (both[count:] + one(left[:count], low))


def dot3t(left, right):
    high, low = right

    def one(a, b):
        return lax.dot_general(a, b, (((1,), (1,)), ((), ())), preferred_element_type=F32)

    count = left.shape[0] // 2
    both = one(left, high)
    return both[:count] + (both[count:] + one(left[:count], low))


def kernel(
    n, n_row,
    offsets, cov_rows, inv_rows, weights, prior, innovation, seen,
    gain_out, shift_out, spread_out,
    land, rows_two, bands, cov_h, cov_l, inv_h, inv_l, ft_h, ft_l,
    x_in, x_keep, w_keep, v_in, v_out, a_hl, pad_hl, acc, pad_acc,
    prior_all, means, f_hl, h_hl, part, vec_in, vec_out,
    g_send, g_recv, r_send, r_recv, s_send, s_recv, p_send, p_recv,
    x_send, x_recv, home_send, home_recv, v_send, v_recv, vec_send, vec_recv,
):
    tm = lax.axis_index("tm")
    row = lax.axis_index("row")
    rows, columns = cov_rows.shape
    tiles = columns // TILE
    even = lax.rem(tm, 2) == 0
    odd = lax.rem(tm, 2) == 1

    def at(index, size):
        return pl.ds(pl.multiple_of(index * size, size), size)

    def remote(src, dst, send, recv, to_tm, to_row):
        return pltpu.make_async_remote_copy(
            src_ref=src, dst_ref=dst, send_sem=send, recv_sem=recv,
            device_id=(to_tm, to_row), device_id_type=MESH,
        )

    barrier = pltpu.get_barrier_semaphore()

    def greet(t, r):
        pl.semaphore_signal(barrier, inc=1, device_id=(t, r), device_id_type=MESH)

    for d in range(1, n_row):
        greet(tm, lax.rem(row + d, n_row))
    for d in range(1, SPAN + 1):
        pl.when(tm + d < n)(lambda d=d: greet(tm + d, row))
        pl.when(tm - d >= 0)(lambda d=d: greet(tm - d, row))
    pl.semaphore_wait(
        barrier, n_row - 1 + jnp.minimum(tm, SPAN) + jnp.minimum(n - 1 - tm, SPAN)
    )

    twin = even & (tm >= 2) & (tm + 2 < n)
    lends = even & (tm >= 4)

    def valid(s):
        last = (odd & (tm >= SPAN)) | twin
        return ((s < SPAN) & (tm >= s)) | ((s == SPAN) & last)

    def goes_on(s):
        return valid(s) & (s < SPAN) & (tm + 1 < n)

    def goes_home(s):
        return valid(s) & (s > 0) & ((s == SPAN) | (tm == n - 1))

    def goes_back(s):
        return valid(s) & (s > 0)

    def chosen(s):
        return jnp.where((s == SPAN) & even, 1, 0)

    square = n_row == 4 and rows == TILE
    half = rows // 2
    if square:
        x, y = lax.rem(row, 2), row // 2
        r1, r2, r3 = 2 * y + 1 - x, 2 * (1 - y) + x, 2 * (1 - y) + 1 - x
        every, low, top = pl.ds(0, rows), pl.ds(0, half), pl.ds(half, half)
        right = pl.ds(pl.multiple_of(row * rows + half, half), half)
        right3 = pl.ds(pl.multiple_of(r3 * rows + half, half), half)
        plan = []
        for slot, to in enumerate((r1, r2, r3)):
            plan.append((to, slot, low, at(row, rows), every))
            plan.append((to, slot, top, right, top))
        plan.append((r1, 3, every, at(r2, rows), every))
        plan.append((r2, 4, every, at(r1, rows), every))
        plan.append((r1, 5, low, at(r3, rows), every))
        plan.append((r2, 6, every, right3, low))
    else:
        every = pl.ds(0, rows)
        wide = pl.ds(0, columns)
        plan = [
            (lax.rem(row + d, n_row), d - 1, every, wide, wide) for d in range(1, n_row)
        ]

    def gather(m, src):
        return [
            remote(
                src.at[rsl, csl], land.at[0, m, slot, rsl, dsl],
                g_send.at[m, c], g_recv.at[m, c], tm, to,
            )
            for c, (to, slot, rsl, csl, dsl) in enumerate(plan)
        ]

    def lend(m):
        return [
            remote(
                land.at[0, m, slot, rsl, dsl], land.at[1, m, slot, rsl, dsl],
                r_send.at[m, c], r_recv.at[m, c], tm - 2, row,
            )
            for c, (to, slot, rsl, csl, dsl) in enumerate(plan)
        ]

    def share():
        return [
            remote(
                rows_two.at[1, rsl, csl], land.at[1, 1, slot, rsl, dsl],
                r_send.at[1, c], r_recv.at[1, c], tm, to,
            )
            for c, (to, slot, rsl, csl, dsl) in enumerate(plan)
        ]

    def small(c, src, dst):
        return remote(src, dst, s_send.at[c], s_recv.at[c], tm - 2, row)

    lend_rows = [
        small(1, cov_rows, rows_two.at[1]), small(0, inv_rows, rows_two.at[0])
    ]
    lend_bands = small(2, bands.at[0], bands.at[1])
    lend_means = small(3, means.at[0], means.at[1])

    def putter(which, high, low_part):
        def put(rsl, csl, value):
            h, l = split(value)
            high[which, rsl, csl] = h
            low_part[which, rsl, csl] = l

        return put

    def fill_own(which, src, high, low_part):
        put = putter(which, high, low_part)
        put(at(row, rows), pl.ds(0, columns), src[...])
        if square:
            for r in (r1, r2, r3):
                put(at(r, rows), at(row, rows), src[:, at(r, rows)].T)

    def fill_slots(which, m, copies, high, low_part, on=None):
        put = putter(which, high, low_part)
        for slot in range(7 if square else n_row - 1):
            for c, entry in enumerate(plan):
                if entry[1] == slot:
                    copies[c].wait_recv()
                    if on is not None:
                        pl.when(lends)(lambda c=c: on[c].start())
            if not square:
                owner = lax.rem(row + n_row - 1 - slot, n_row)
                put(at(owner, rows), pl.ds(0, columns), land[which, m, slot])
            elif slot < 3:
                r = (r1, r2, r3)[slot]
                upper = pl.ds(pl.multiple_of(r * rows, half), half)
                lower = pl.ds(pl.multiple_of(r * rows + half, half), half)
                put(upper, at(r, rows), land[which, m, slot, :half, :])
                put(lower, lower, land[which, m, slot, half:, half:])
                put(lower, upper, land[which, m, slot, :half, half:].T)
            elif slot < 5:
                r = r1 if slot == 3 else r2
                block = land[which, m, slot]
                put(at(r, rows), at(r3, rows), block)
                put(at(r3, rows), at(r, rows), block.T)
            else:
                upper = pl.ds(pl.multiple_of(r1 * rows, half), half)
                lower = pl.ds(pl.multiple_of(r1 * rows + half, half), half)
                if slot == 5:
                    block = land[which, m, 5, :half, :]
                    put(upper, at(r2, rows), block)
                    put(at(r2, rows), upper, block.T)
                else:
                    block = land[which, m, 6, :, :half]
                    put(at(r2, rows), lower, block)
                    put(lower, at(r2, rows), block.T)

    inv_copies = gather(0, inv_rows)
    cov_copies = gather(1, cov_rows)
    for c in inv_copies:
        c.start()

    bands[0] = jnp.zeros(bands.shape[1:], F32)
    bands[0, :NBAND, :] = weights[...]
    for b in range(NBAND):
        bands[0, 8 + b : 9 + b, :] = jnp.full((1, columns), offsets[0, b].astype(F32))

    @pl.when(lends)
    def _():
        lend_bands.start()
        for c in lend_rows:
            c.start()

    vec_out[0] = jnp.broadcast_to(prior[...], (VEC, rows))
    prior_all[row] = vec_out[0]
    prior_copies = [
        remote(
            vec_out.at[0], prior_all.at[row], p_send.at[d - 1], p_recv.at[d - 1],
            tm, lax.rem(row + d, n_row),
        )
        for d in range(1, n_row)
    ]
    for c in prior_copies:
        c.start()

    window = TILE + 2 * EDGE

    def windows(which):
        apart = lax.broadcasted_iota(jnp.int32, (window, TILE), 0) - (
            lax.broadcasted_iota(jnp.int32, (window, TILE), 1) + EDGE
        )
        apart = apart.astype(F32)
        for t in range(tiles):
            cols = slice(t * TILE, (t + 1) * TILE)
            total = jnp.zeros((window, TILE), F32)
            for b in range(NBAND):
                hit = apart == bands[which, 8 + b : 9 + b, cols]
                total = total + jnp.where(hit, bands[which, b : b + 1, cols], 0.0)
            h, l = split(total)
            ft_h[which, t] = h
            ft_l[which, t] = l

    windows(0)

    zeros = jnp.zeros((rows, EDGE), BF16)
    for first in (0, rows):
        pad_hl[first : first + rows, :EDGE] = zeros
        pad_hl[first : first + rows, EDGE + columns :] = zeros

    def full(t):
        return pl.ds(pl.multiple_of(t * TILE, TILE), TILE)

    def x_copy(s, t):
        to = jnp.where((s == SPAN - 1) & odd, tm - 1, tm + 1)
        return remote(
            x_keep.at[s, :, full(t)], x_in.at[s, :, full(t)],
            x_send.at[s, t], x_recv.at[s, t], to, row,
        )

    def home_copy(s, t):
        to = tm - jnp.where((s == SPAN) & even, 1, s)
        return remote(
            x_keep.at[s, :, full(t)], gain_out.at[:, full(t)],
            home_send.at[s, t], home_recv.at[t], to, row,
        )

    def back_to(s):
        return jnp.where((s == SPAN) & even, tm + 1, tm - 1)

    def v_copy(s, t):
        return remote(
            v_out.at[s - 1, :, full(t)], v_in.at[s - 1, :, full(t)],
            v_send.at[s, t], v_recv.at[s, t], back_to(s), row,
        )

    def vec_copy(s):
        return remote(
            vec_out.at[s], vec_in.at[s], vec_send.at[s], vec_recv.at[s], back_to(s), row
        )

    pair = 2 * TILE

    def two(c):
        return pl.ds(pl.multiple_of(c * pair, pair), pair)

    def band_step(s, which):
        h, l = split(w_keep[s])
        pad_hl[:rows, EDGE : EDGE + columns] = h
        pad_hl[rows:, EDGE : EDGE + columns] = l
        for t in range(tiles):
            wide = slice(t * TILE, t * TILE + window)
            cols = slice(t * TILE, (t + 1) * TILE)
            h, l = split(dot3(pad_hl[:, wide], (ft_h[which, t], ft_l[which, t])))
            a_hl[:rows, cols] = h
            a_hl[rows:, cols] = l

    def gain_step(s, which):
        def one(c, carry):
            x_keep[s, :, two(c)] = dot3(
                a_hl[...], (inv_h[which, :, two(c)], inv_l[which, :, two(c)])
            )
            for i in range(2):
                t = 2 * c + i
                pl.when(goes_on(s))(lambda t=t: x_copy(s, t).start())
                early = goes_home(s) & ((s < SPAN) | even | (t < tiles // 2))
                pl.when(early)(lambda t=t: home_copy(s, t).start())
            return carry

        lax.fori_loop(0, tiles // 2, one, 0)

    w_keep[0] = cov_rows[...]
    band_step(0, 0)
    fill_own(0, inv_rows, inv_h, inv_l)
    fill_own(0, cov_rows, cov_h, cov_l)
    ahead = len(plan) - 4 if square else len(plan)
    for c in inv_copies[:ahead]:
        c.wait_send()
    for c in cov_copies:
        c.start()
    fill_slots(0, 0, inv_copies, inv_h, inv_l, lend(0))
    gain_step(0, 0)

    @pl.when(tm == n - 1)
    def _():
        gain_out[...] = x_keep[0]

    count = seen.shape[1]
    spots = jnp.broadcast_to(seen[...].astype(F32), (count, count)).T
    lanes = lax.broadcasted_iota(jnp.int32, (count, count), 1).astype(F32)
    matches = jnp.concatenate(
        [
            jnp.where(lanes + float(c * count) == spots, 1.0, 0.0)
            for c in range(columns // count)
        ],
        axis=1,
    ).astype(BF16)
    values = jnp.broadcast_to(innovation[...], (VEC, count))
    first, second = split(values)
    third = (values - first.astype(F32) - second.astype(F32)).astype(BF16)
    total = jnp.zeros((VEC, columns), F32)
    for piece in (third, second, first):
        total = total + jnp.dot(piece, matches, preferred_element_type=F32)
    pulled = stack(total)
    own = vec_out[0] + dot3t(pulled, split(cov_rows[...]))
    for c in prior_copies:
        c.wait()
    @pl.when(twin)
    def _():
        lend_bands.wait_recv()
        windows(1)
        for c in lend_rows:
            c.wait_recv()
        fill_own(1, rows_two.at[1], cov_h, cov_l)
        fill_own(1, rows_two.at[0], inv_h, inv_l)

    for c in inv_copies[ahead:] + cov_copies:
        c.wait_send()

    @pl.when(twin)
    def _():
        for c in share():
            c.start()

    fill_slots(0, 1, cov_copies, cov_h, cov_l)
    inside = slice(EDGE, EDGE + columns)

    def cut_means(which):
        zeros = jnp.zeros((2 * VEC, EDGE), BF16)
        f_hl[which, :, :EDGE] = zeros
        f_hl[which, :, EDGE + columns :] = zeros
        f_hl[which, :, inside] = stack(means[which, 0])

    def cut_moved(which):
        h_hl[which] = stack(means[which, 1])

    def filtered():
        prior_row = jnp.concatenate([prior_all[r] for r in range(n_row)], axis=1)
        for t in range(tiles):
            cols = slice(t * TILE, (t + 1) * TILE)
            means[0, 0, :, cols] = prior_row[:, cols] + dot3(
                pulled, (cov_h[0, :, cols], cov_l[0, :, cols])
            )
        cut_means(0)
        for t in range(tiles):
            wide = slice(t * TILE, t * TILE + window)
            means[0, 1, :, t * TILE : (t + 1) * TILE] = dot3(
                f_hl[0, :, wide], (ft_h[0, t], ft_l[0, t])
            )
        cut_moved(0)
        pl.when(lends)(lambda: lend_means.start())

    def moved_part(s, which):
        return dot3t(h_hl[which], split(x_keep[s]))

    def forward(i, carry):
        s = jnp.where(twin & (i > 1), SPAN + 2 - i, i)
        which = chosen(s)

        @pl.when(twin & (s == SPAN))
        def _():
            lend_means.wait_recv()
            cut_means(1)
            cut_moved(1)

        @pl.when(valid(s))
        def _():
            w_keep[s] = jnp.zeros((rows, columns), F32)

            def one(t, carry):
                x_copy(s - 1, t).wait_recv()
                piece = stack(x_in[s - 1, :, full(t)])
                for c in range(0, columns, 2 * TILE):
                    cols = slice(c, c + 2 * TILE)
                    w_keep[s, :, cols] += dot3(
                        piece, (cov_h[which, full(t), cols], cov_l[which, full(t), cols])
                    )
                return carry

            lax.fori_loop(0, tiles, one, 0)
            band_step(s, which)
            gain_step(s, which)

        @pl.when(s == 1)
        def _():
            filtered()
            part[0] = own - moved_part(0, 0)

        @pl.when(valid(s))
        def _():
            part[s] = dot3t(f_hl[which, :, inside], split(x_in[s - 1])) - moved_part(s, which)

        @pl.when(twin & (s == 1))
        def _():
            fill_slots(1, 0, lend(0), inv_h, inv_l)
            fill_slots(1, 1, share(), cov_h, cov_l)

        return carry

    lax.fori_loop(1, SPAN + 1, forward, 0)

    def backward(i, carry):
        s = SPAN - i
        which = chosen(s)

        @pl.when(valid(s))
        def _():
            acc[...] = -x_keep[s]
            vec_out[s] = part[s]

            @pl.when((s < SPAN) & (tm < n - 1))
            def _():
                def one(t, carry):
                    v_copy(s + 1, t).wait_recv()
                    piece = stack(v_in[s, :, full(t)])
                    for c in range(0, columns, 2 * TILE):
                        cols = slice(c, c + 2 * TILE)
                        acc[:, cols] += dot3(
                            piece, (inv_h[0, full(t), cols], inv_l[0, full(t), cols])
                        )
                    return carry

                lax.fori_loop(0, tiles, one, 0)
                vec_copy(s + 1).wait_recv()
                vec_out[s] += vec_in[s + 1]

            pl.when(goes_back(s))(lambda: vec_copy(s).start())
            pad_acc[...] = jnp.zeros(pad_acc.shape, F32)
            for t in range(tiles):
                wide = slice(t * TILE, t * TILE + window)
                piece = stack(acc[:, t * TILE : (t + 1) * TILE])
                pad_acc[:, wide] += dot3t(piece, (ft_h[which, t], ft_l[which, t]))
            h, l = split(pad_acc[:, inside])
            a_hl[:rows] = h
            a_hl[rows:] = l

            def last(c, carry):
                value = w_keep[s, :, two(c)] + dot3(
                    a_hl[...], (cov_h[which, :, two(c)], cov_l[which, :, two(c)])
                )

                @pl.when(s > 0)
                def _():
                    v_out[s - 1, :, two(c)] = value
                    for i in range(2):
                        v_copy(s, 2 * c + i).start()

                @pl.when(s == 0)
                def _():
                    spread_out[:, two(c)] = value

                return carry

            lax.fori_loop(0, tiles // 2, last, 0)

        @pl.when((s == 1) & odd & valid(SPAN))
        def _():
            for t in range(tiles // 2, tiles):
                home_copy(SPAN, t).start()

        return carry

    lax.fori_loop(0, SPAN + 1, backward, 0)
    shift_out[...] = vec_out[0, :1, :]

    @pl.when(tm < n - 1)
    def _():
        for t in range(tiles):
            home_copy(1, t).wait_recv()

    @pl.when(lends)
    def _():
        for c in lend_rows + [lend_bands, lend_means] + lend(0):
            c.wait_send()

    @pl.when(twin)
    def _():
        for c in share():
            c.wait_send()

    for s in range(SPAN + 1):
        if s > 0:
            pl.when(goes_back(s))(lambda s=s: vec_copy(s).wait_send())
        for t in range(tiles):
            if s < SPAN:
                pl.when(goes_on(s))(lambda s=s, t=t: x_copy(s, t).wait_send())
            if s > 0:
                pl.when(goes_home(s))(lambda s=s, t=t: home_copy(s, t).wait_send())
                pl.when(goes_back(s))(lambda s=s, t=t: v_copy(s, t).wait_send())


def body(n, n_row, covariance, precision, band_weight, band_offset, prior_mean, innovation, seen_sites):
    rows, columns = covariance.shape[1:]
    tiles = columns // TILE
    window = TILE + 2 * EDGE
    steps = SPAN + 1
    square = n_row == 4 and rows == TILE
    copies = 10 if square else n_row - 1
    slots = (7, rows, rows) if square else (n_row - 1, rows, columns)
    block = lambda *lead: pltpu.VMEM(lead + (rows, columns), F32)
    whole = pltpu.VMEM((2, columns, columns), BF16)
    vec = lambda *lead: pltpu.VMEM(lead + (VEC, rows), F32)
    padded = columns + 2 * EDGE
    dma = lambda *shape: pltpu.SemaphoreType.DMA(shape)
    vmem = pl.BlockSpec(memory_space=pltpu.VMEM)
    gain, shift, spread = pl.pallas_call(
        functools.partial(kernel, n, n_row),
        out_shape=(
            jax.ShapeDtypeStruct((rows, columns), F32),
            jax.ShapeDtypeStruct((1, rows), F32),
            jax.ShapeDtypeStruct((rows, columns), F32),
        ),
        in_specs=[pl.BlockSpec(memory_space=pltpu.SMEM)] + [vmem] * 6,
        out_specs=(vmem, vmem, vmem),
        scratch_shapes=[
            pltpu.VMEM((2, 2) + slots, F32), block(2), pltpu.VMEM((2, 16, columns), F32),
            whole, whole, whole, whole,
            pltpu.VMEM((2, tiles, window, TILE), BF16), pltpu.VMEM((2, tiles, window, TILE), BF16),
            block(SPAN), block(steps), block(steps), block(SPAN), block(SPAN),
            pltpu.VMEM((2 * rows, columns), BF16), pltpu.VMEM((2 * rows, padded), BF16),
            block(), pltpu.VMEM((rows, padded), F32),
            vec(n_row), pltpu.VMEM((2, 2, VEC, columns), F32),
            pltpu.VMEM((2, 2 * VEC, padded), BF16), pltpu.VMEM((2, 2 * VEC, columns), BF16),
            vec(steps), vec(steps), vec(steps),
            dma(2, copies), dma(2, copies), dma(2, copies), dma(2, copies), dma(4), dma(4),
            dma(n_row - 1), dma(n_row - 1),
            dma(SPAN, tiles), dma(SPAN, tiles), dma(steps, tiles), dma(tiles),
            dma(steps, tiles), dma(steps, tiles), dma(steps), dma(steps),
        ],
        compiler_params=pltpu.CompilerParams(
            collective_id=0, has_side_effects=True, vmem_limit_bytes=62 * 2**20
        ),
        cost_estimate=pl.CostEstimate(
            flops=2 * 54 * rows * columns * columns, bytes_accessed=16 * rows * columns,
            transcendentals=0,
        ),
    )(
        band_offset, covariance[0], precision[0], band_weight[0],
        prior_mean, innovation, seen_sites,
    )
    return gain[None], shift, spread[None]


def solution(mesh):
    in_specs = (
        P("tm", "row", None),
        P("tm", "row", None),
        P("tm", None, None),
        P("tm", None),
        P("tm", "row"),
        P("tm", None),
        P("tm", None),
    )
    out_specs = (P("tm", "row", None), P("tm", "row"), P("tm", "row", None))
    return jax.shard_map(
        functools.partial(body, mesh.shape["tm"], mesh.shape["row"]),
        mesh=mesh, in_specs=in_specs, out_specs=out_specs, check_vma=False,
    )
```

```python
import functools

import jax
import jax.numpy as jnp
from jax import lax
from jax.experimental import pallas as pl
from jax.experimental.pallas import tpu as pltpu
from jax.sharding import PartitionSpec as P

NBAND = 5
REACH = 64
SPAN = 3
TILE = 256
EDGE = 128
VEC = 16

MESH = pl.DeviceIdType.MESH
F32 = jnp.float32
BF16 = jnp.bfloat16


def split(value):
    high = value.astype(BF16)
    return high, (value - high.astype(F32)).astype(BF16)


def stack(value):
    return jnp.concatenate(split(value), axis=0)


def dot3(left, right):
    high, low = right
    one = functools.partial(jnp.dot, preferred_element_type=F32)
    count = left.shape[0] // 2
    top, rest = left[:count], left[count:]
    return one(top, high) + (one(top, low) + one(rest, high))


def dot3t(left, right):
    high, low = right

    def one(a, b):
        return lax.dot_general(a, b, (((1,), (1,)), ((), ())), preferred_element_type=F32)

    count = left.shape[0] // 2
    top, rest = left[:count], left[count:]
    return one(top, high) + (one(top, low) + one(rest, high))


def kernel(
    n, n_row,
    offsets, cov_rows, inv_rows, weights, prior, innovation, seen,
    gain_out, shift_out, spread_out,
    land, rows_two, bands, cov_h, cov_l, inv_h, inv_l, ft_h, ft_l,
    x_in, x_keep, w_keep, v_in, v_out, a_hl, pad_hl, acc, pad_acc,
    prior_all, means, f_hl, h_hl, part, vec_in, vec_out,
    g_send, g_recv, r_send, r_recv, s_send, s_recv, p_send, p_recv,
    x_send, x_recv, home_send, home_recv, v_send, v_recv, vec_send, vec_recv,
):
    tm = lax.axis_index("tm")
    row = lax.axis_index("row")
    rows, columns = cov_rows.shape
    tiles = columns // TILE
    even = lax.rem(tm, 2) == 0
    odd = lax.rem(tm, 2) == 1

    def at(index, size):
        return pl.ds(pl.multiple_of(index * size, size), size)

    def remote(src, dst, send, recv, to_tm, to_row):
        return pltpu.make_async_remote_copy(
            src_ref=src, dst_ref=dst, send_sem=send, recv_sem=recv,
            device_id=(to_tm, to_row), device_id_type=MESH,
        )

    barrier = pltpu.get_barrier_semaphore()

    def greet(t, r):
        pl.semaphore_signal(barrier, inc=1, device_id=(t, r), device_id_type=MESH)

    for d in range(1, n_row):
        greet(tm, lax.rem(row + d, n_row))
    for d in range(1, SPAN + 1):
        pl.when(tm + d < n)(lambda d=d: greet(tm + d, row))
        pl.when(tm - d >= 0)(lambda d=d: greet(tm - d, row))
    pl.semaphore_wait(
        barrier, n_row - 1 + jnp.minimum(tm, SPAN) + jnp.minimum(n - 1 - tm, SPAN)
    )

    twin = even & (tm >= 2) & (tm + 2 < n)
    lends = even & (tm >= 4)

    def valid(s):
        last = (odd & (tm >= SPAN)) | twin
        return ((s < SPAN) & (tm >= s)) | ((s == SPAN) & last)

    def goes_on(s):
        return valid(s) & (s < SPAN) & (tm + 1 < n)

    def goes_home(s):
        return valid(s) & (s > 0) & ((s == SPAN) | (tm == n - 1))

    def goes_back(s):
        return valid(s) & (s > 0)

    def chosen(s):
        return jnp.where((s == SPAN) & even, 1, 0)

    square = n_row == 4 and rows == TILE
    half = rows // 2
    if square:
        x, y = lax.rem(row, 2), row // 2
        r1, r2, r3 = 2 * y + 1 - x, 2 * (1 - y) + x, 2 * (1 - y) + 1 - x
        every, low, top = pl.ds(0, rows), pl.ds(0, half), pl.ds(half, half)
        right = pl.ds(pl.multiple_of(row * rows + half, half), half)
        right3 = pl.ds(pl.multiple_of(r3 * rows + half, half), half)
        plan = []
        for slot, to in enumerate((r1, r2, r3)):
            plan.append((to, slot, low, at(row, rows), every))
            plan.append((to, slot, top, right, top))
        plan.append((r1, 3, every, at(r2, rows), every))
        plan.append((r2, 4, every, at(r1, rows), every))
        plan.append((r1, 5, low, at(r3, rows), every))
        plan.append((r2, 6, every, right3, low))
    else:
        every = pl.ds(0, rows)
        wide = pl.ds(0, columns)
        plan = [
            (lax.rem(row + d, n_row), d - 1, every, wide, wide) for d in range(1, n_row)
        ]

    def gather(m, src):
        return [
            remote(
                src.at[rsl, csl], land.at[0, m, slot, rsl, dsl],
                g_send.at[m, c], g_recv.at[m, c], tm, to,
            )
            for c, (to, slot, rsl, csl, dsl) in enumerate(plan)
        ]

    def lend(m):
        return [
            remote(
                land.at[0, m, slot, rsl, dsl], land.at[1, m, slot, rsl, dsl],
                r_send.at[m, c], r_recv.at[m, c], tm - 2, row,
            )
            for c, (to, slot, rsl, csl, dsl) in enumerate(plan)
        ]

    def share():
        return [
            remote(
                rows_two.at[1, rsl, csl], land.at[1, 1, slot, rsl, dsl],
                r_send.at[1, c], r_recv.at[1, c], tm, to,
            )
            for c, (to, slot, rsl, csl, dsl) in enumerate(plan)
        ]

    def small(c, src, dst):
        return remote(src, dst, s_send.at[c], s_recv.at[c], tm - 2, row)

    lend_rows = [
        small(1, cov_rows, rows_two.at[1]), small(0, inv_rows, rows_two.at[0])
    ]
    lend_bands = small(2, bands.at[0], bands.at[1])
    lend_means = small(3, means.at[0], means.at[1])

    def putter(which, high, low_part):
        def put(rsl, csl, value):
            h, l = split(value)
            high[which, rsl, csl] = h
            low_part[which, rsl, csl] = l

        return put

    def fill_own(which, src, high, low_part):
        put = putter(which, high, low_part)
        put(at(row, rows), pl.ds(0, columns), src[...])
        if square:
            for r in (r1, r2, r3):
                put(at(r, rows), at(row, rows), src[:, at(r, rows)].T)

    def fill_slots(which, m, copies, high, low_part, on=None):
        put = putter(which, high, low_part)
        for slot in range(7 if square else n_row - 1):
            for c, entry in enumerate(plan):
                if entry[1] == slot:
                    copies[c].wait_recv()
                    if on is not None:
                        pl.when(lends)(lambda c=c: on[c].start())
            if not square:
                owner = lax.rem(row + n_row - 1 - slot, n_row)
                put(at(owner, rows), pl.ds(0, columns), land[which, m, slot])
            elif slot < 3:
                r = (r1, r2, r3)[slot]
                upper = pl.ds(pl.multiple_of(r * rows, half), half)
                lower = pl.ds(pl.multiple_of(r * rows + half, half), half)
                put(upper, at(r, rows), land[which, m, slot, :half, :])
                put(lower, lower, land[which, m, slot, half:, half:])
                put(lower, upper, land[which, m, slot, :half, half:].T)
            elif slot < 5:
                r = r1 if slot == 3 else r2
                block = land[which, m, slot]
                put(at(r, rows), at(r3, rows), block)
                put(at(r3, rows), at(r, rows), block.T)
            else:
                upper = pl.ds(pl.multiple_of(r1 * rows, half), half)
                lower = pl.ds(pl.multiple_of(r1 * rows + half, half), half)
                if slot == 5:
                    block = land[which, m, 5, :half, :]
                    put(upper, at(r2, rows), block)
                    put(at(r2, rows), upper, block.T)
                else:
                    block = land[which, m, 6, :, :half]
                    put(at(r2, rows), lower, block)
                    put(lower, at(r2, rows), block.T)

    inv_copies = gather(0, inv_rows)
    cov_copies = gather(1, cov_rows)
    for c in inv_copies:
        c.start()

    bands[0] = jnp.zeros(bands.shape[1:], F32)
    bands[0, :NBAND, :] = weights[...]
    for b in range(NBAND):
        bands[0, 8 + b : 9 + b, :] = jnp.full((1, columns), offsets[0, b].astype(F32))

    @pl.when(lends)
    def _():
        lend_bands.start()
        for c in lend_rows:
            c.start()

    vec_out[0] = jnp.broadcast_to(prior[...], (VEC, rows))
    prior_all[row] = vec_out[0]
    prior_copies = [
        remote(
            vec_out.at[0], prior_all.at[row], p_send.at[d - 1], p_recv.at[d - 1],
            tm, lax.rem(row + d, n_row),
        )
        for d in range(1, n_row)
    ]
    for c in prior_copies:
        c.start()

    window = TILE + 2 * EDGE

    def windows(which):
        apart = lax.broadcasted_iota(jnp.int32, (window, TILE), 0) - (
            lax.broadcasted_iota(jnp.int32, (window, TILE), 1) + EDGE
        )
        apart = apart.astype(F32)
        for t in range(tiles):
            cols = slice(t * TILE, (t + 1) * TILE)
            total = jnp.zeros((window, TILE), F32)
            for b in range(NBAND):
                hit = apart == bands[which, 8 + b : 9 + b, cols]
                total = total + jnp.where(hit, bands[which, b : b + 1, cols], 0.0)
            h, l = split(total)
            ft_h[which, t] = h
            ft_l[which, t] = l

    windows(0)

    zeros = jnp.zeros((rows, EDGE), BF16)
    for first in (0, rows):
        pad_hl[first : first + rows, :EDGE] = zeros
        pad_hl[first : first + rows, EDGE + columns :] = zeros

    def full(t):
        return pl.ds(pl.multiple_of(t * TILE, TILE), TILE)

    def x_copy(s, t):
        to = jnp.where((s == SPAN - 1) & odd, tm - 1, tm + 1)
        return remote(
            x_keep.at[s, :, full(t)], x_in.at[s, :, full(t)],
            x_send.at[s, t], x_recv.at[s, t], to, row,
        )

    def home_copy(s, t):
        to = tm - jnp.where((s == SPAN) & even, 1, s)
        return remote(
            x_keep.at[s, :, full(t)], gain_out.at[:, full(t)],
            home_send.at[s, t], home_recv.at[t], to, row,
        )

    def back_to(s):
        return jnp.where((s == SPAN) & even, tm + 1, tm - 1)

    def v_copy(s, t):
        return remote(
            v_out.at[s - 1, :, full(t)], v_in.at[s - 1, :, full(t)],
            v_send.at[s, t], v_recv.at[s, t], back_to(s), row,
        )

    def vec_copy(s):
        return remote(
            vec_out.at[s], vec_in.at[s], vec_send.at[s], vec_recv.at[s], back_to(s), row
        )

    pair = 2 * TILE

    def two(c):
        return pl.ds(pl.multiple_of(c * pair, pair), pair)

    def band_step(s, which):
        h, l = split(w_keep[s])
        pad_hl[:rows, EDGE : EDGE + columns] = h
        pad_hl[rows:, EDGE : EDGE + columns] = l
        for t in range(tiles):
            wide = slice(t * TILE, t * TILE + window)
            cols = slice(t * TILE, (t + 1) * TILE)
            h, l = split(dot3(pad_hl[:, wide], (ft_h[which, t], ft_l[which, t])))
            a_hl[:rows, cols] = h
            a_hl[rows:, cols] = l

    def gain_step(s, which):
        def one(c, carry):
            x_keep[s, :, two(c)] = dot3(
                a_hl[...], (inv_h[which, :, two(c)], inv_l[which, :, two(c)])
            )
            for i in range(2):
                t = 2 * c + i
                pl.when(goes_on(s))(lambda t=t: x_copy(s, t).start())
                early = goes_home(s) & ((s < SPAN) | (t < tiles // 2))
                pl.when(early)(lambda t=t: home_copy(s, t).start())
            return carry

        lax.fori_loop(0, tiles // 2, one, 0)

    w_keep[0] = cov_rows[...]
    band_step(0, 0)
    fill_own(0, inv_rows, inv_h, inv_l)
    fill_own(0, cov_rows, cov_h, cov_l)
    ahead = len(plan) - 4 if square else len(plan)
    for c in inv_copies[:ahead]:
        c.wait_send()
    for c in cov_copies:
        c.start()
    fill_slots(0, 0, inv_copies, inv_h, inv_l, lend(0))
    gain_step(0, 0)

    @pl.when(tm == n - 1)
    def _():
        gain_out[...] = x_keep[0]

    count = seen.shape[1]
    spots = jnp.broadcast_to(seen[...].astype(F32), (count, count)).T
    lanes = lax.broadcasted_iota(jnp.int32, (count, count), 1).astype(F32)
    matches = jnp.concatenate(
        [
            jnp.where(lanes + float(c * count) == spots, 1.0, 0.0)
            for c in range(columns // count)
        ],
        axis=1,
    ).astype(BF16)
    values = jnp.broadcast_to(innovation[...], (VEC, count))
    first, second = split(values)
    third = (values - first.astype(F32) - second.astype(F32)).astype(BF16)
    total = jnp.zeros((VEC, columns), F32)
    for piece in (third, second, first):
        total = total + jnp.dot(piece, matches, preferred_element_type=F32)
    pulled = stack(total)
    own = vec_out[0] + dot3t(pulled, split(cov_rows[...]))
    for c in prior_copies:
        c.wait()
    for c in inv_copies[ahead:] + cov_copies:
        c.wait_send()

    @pl.when(twin)
    def _():
        lend_rows[0].wait_recv()
        for c in share():
            c.start()

    fill_slots(0, 1, cov_copies, cov_h, cov_l)
    inside = slice(EDGE, EDGE + columns)

    def cut_means(which):
        zeros = jnp.zeros((2 * VEC, EDGE), BF16)
        f_hl[which, :, :EDGE] = zeros
        f_hl[which, :, EDGE + columns :] = zeros
        f_hl[which, :, inside] = stack(means[which, 0])

    def cut_moved(which):
        h_hl[which] = stack(means[which, 1])

    def filtered():
        prior_row = jnp.concatenate([prior_all[r] for r in range(n_row)], axis=1)
        for t in range(tiles):
            cols = slice(t * TILE, (t + 1) * TILE)
            means[0, 0, :, cols] = prior_row[:, cols] + dot3(
                pulled, (cov_h[0, :, cols], cov_l[0, :, cols])
            )
        cut_means(0)
        for t in range(tiles):
            wide = slice(t * TILE, t * TILE + window)
            means[0, 1, :, t * TILE : (t + 1) * TILE] = dot3(
                f_hl[0, :, wide], (ft_h[0, t], ft_l[0, t])
            )
        cut_moved(0)
        pl.when(lends)(lambda: lend_means.start())

    def moved_part(s, which):
        return dot3t(h_hl[which], split(x_keep[s]))

    def forward(s, carry):
        which = chosen(s)

        @pl.when(twin & (s == SPAN))
        def _():
            lend_means.wait_recv()
            cut_means(1)
            cut_moved(1)

        @pl.when(valid(s))
        def _():
            w_keep[s] = jnp.zeros((rows, columns), F32)

            def one(t, carry):
                x_copy(s - 1, t).wait_recv()
                piece = stack(x_in[s - 1, :, full(t)])
                for c in range(0, columns, 2 * TILE):
                    cols = slice(c, c + 2 * TILE)
                    w_keep[s, :, cols] += dot3(
                        piece, (cov_h[which, full(t), cols], cov_l[which, full(t), cols])
                    )
                return carry

            lax.fori_loop(0, tiles, one, 0)
            band_step(s, which)
            gain_step(s, which)

        @pl.when(s == 1)
        def _():
            filtered()
            part[0] = own - moved_part(0, 0)

        @pl.when(valid(s))
        def _():
            part[s] = dot3t(f_hl[which, :, inside], split(x_in[s - 1])) - moved_part(s, which)

        @pl.when(twin & (s == 1))
        def _():
            lend_bands.wait_recv()
            windows(1)
            lend_rows[1].wait_recv()
            fill_own(1, rows_two.at[0], inv_h, inv_l)
            fill_slots(1, 0, lend(0), inv_h, inv_l)
            fill_own(1, rows_two.at[1], cov_h, cov_l)
            fill_slots(1, 1, share(), cov_h, cov_l)

        return carry

    lax.fori_loop(1, SPAN + 1, forward, 0)

    def backward(i, carry):
        s = SPAN - i
        which = chosen(s)

        @pl.when(valid(s))
        def _():
            acc[...] = -x_keep[s]
            vec_out[s] = part[s]

            @pl.when((s < SPAN) & (tm < n - 1))
            def _():
                def one(t, carry):
                    v_copy(s + 1, t).wait_recv()
                    piece = stack(v_in[s, :, full(t)])
                    for c in range(0, columns, 2 * TILE):
                        cols = slice(c, c + 2 * TILE)
                        acc[:, cols] += dot3(
                            piece, (inv_h[0, full(t), cols], inv_l[0, full(t), cols])
                        )
                    return carry

                lax.fori_loop(0, tiles, one, 0)
                vec_copy(s + 1).wait_recv()
                vec_out[s] += vec_in[s + 1]

            pl.when(goes_back(s))(lambda: vec_copy(s).start())
            pad_acc[...] = jnp.zeros(pad_acc.shape, F32)
            for t in range(tiles):
                wide = slice(t * TILE, t * TILE + window)
                piece = stack(acc[:, t * TILE : (t + 1) * TILE])
                pad_acc[:, wide] += dot3t(piece, (ft_h[which, t], ft_l[which, t]))
            h, l = split(pad_acc[:, inside])
            a_hl[:rows] = h
            a_hl[rows:] = l

            def last(c, carry):
                value = w_keep[s, :, two(c)] + dot3(
                    a_hl[...], (cov_h[which, :, two(c)], cov_l[which, :, two(c)])
                )

                @pl.when(s > 0)
                def _():
                    v_out[s - 1, :, two(c)] = value
                    for i in range(2):
                        v_copy(s, 2 * c + i).start()

                @pl.when(s == 0)
                def _():
                    spread_out[:, two(c)] = value

                return carry

            lax.fori_loop(0, tiles // 2, last, 0)

        @pl.when((s == 1) & valid(SPAN))
        def _():
            for t in range(tiles // 2, tiles):
                home_copy(SPAN, t).start()

        return carry

    lax.fori_loop(0, SPAN + 1, backward, 0)
    shift_out[...] = vec_out[0, :1, :]

    @pl.when(tm < n - 1)
    def _():
        for t in range(tiles):
            home_copy(1, t).wait_recv()

    @pl.when(lends)
    def _():
        for c in lend_rows + [lend_bands, lend_means] + lend(0):
            c.wait_send()

    @pl.when(twin)
    def _():
        for c in share():
            c.wait_send()

    for s in range(SPAN + 1):
        if s > 0:
            pl.when(goes_back(s))(lambda s=s: vec_copy(s).wait_send())
        for t in range(tiles):
            if s < SPAN:
                pl.when(goes_on(s))(lambda s=s, t=t: x_copy(s, t).wait_send())
            if s > 0:
                pl.when(goes_home(s))(lambda s=s, t=t: home_copy(s, t).wait_send())
                pl.when(goes_back(s))(lambda s=s, t=t: v_copy(s, t).wait_send())


def body(n, n_row, covariance, precision, band_weight, band_offset, prior_mean, innovation, seen_sites):
    rows, columns = covariance.shape[1:]
    tiles = columns // TILE
    window = TILE + 2 * EDGE
    steps = SPAN + 1
    square = n_row == 4 and rows == TILE
    copies = 10 if square else n_row - 1
    slots = (7, rows, rows) if square else (n_row - 1, rows, columns)
    block = lambda *lead: pltpu.VMEM(lead + (rows, columns), F32)
    whole = pltpu.VMEM((2, columns, columns), BF16)
    vec = lambda *lead: pltpu.VMEM(lead + (VEC, rows), F32)
    padded = columns + 2 * EDGE
    dma = lambda *shape: pltpu.SemaphoreType.DMA(shape)
    vmem = pl.BlockSpec(memory_space=pltpu.VMEM)
    gain, shift, spread = pl.pallas_call(
        functools.partial(kernel, n, n_row),
        out_shape=(
            jax.ShapeDtypeStruct((rows, columns), F32),
            jax.ShapeDtypeStruct((1, rows), F32),
            jax.ShapeDtypeStruct((rows, columns), F32),
        ),
        in_specs=[pl.BlockSpec(memory_space=pltpu.SMEM)] + [vmem] * 6,
        out_specs=(vmem, vmem, vmem),
        scratch_shapes=[
            pltpu.VMEM((2, 2) + slots, F32), block(2), pltpu.VMEM((2, 16, columns), F32),
            whole, whole, whole, whole,
            pltpu.VMEM((2, tiles, window, TILE), BF16), pltpu.VMEM((2, tiles, window, TILE), BF16),
            block(SPAN), block(steps), block(steps), block(SPAN), block(SPAN),
            pltpu.VMEM((2 * rows, columns), BF16), pltpu.VMEM((2 * rows, padded), BF16),
            block(), pltpu.VMEM((rows, padded), F32),
            vec(n_row), pltpu.VMEM((2, 2, VEC, columns), F32),
            pltpu.VMEM((2, 2 * VEC, padded), BF16), pltpu.VMEM((2, 2 * VEC, columns), BF16),
            vec(steps), vec(steps), vec(steps),
            dma(2, copies), dma(2, copies), dma(2, copies), dma(2, copies), dma(4), dma(4),
            dma(n_row - 1), dma(n_row - 1),
            dma(SPAN, tiles), dma(SPAN, tiles), dma(steps, tiles), dma(tiles),
            dma(steps, tiles), dma(steps, tiles), dma(steps), dma(steps),
        ],
        compiler_params=pltpu.CompilerParams(
            collective_id=0, has_side_effects=True, vmem_limit_bytes=62 * 2**20
        ),
        cost_estimate=pl.CostEstimate(
            flops=2 * 54 * rows * columns * columns, bytes_accessed=16 * rows * columns,
            transcendentals=0,
        ),
    )(
        band_offset, covariance[0], precision[0], band_weight[0],
        prior_mean, innovation, seen_sites,
    )
    return gain[None], shift, spread[None]


def solution(mesh):
    in_specs = (
        P("tm", "row", None),
        P("tm", "row", None),
        P("tm", None, None),
        P("tm", None),
        P("tm", "row"),
        P("tm", None),
        P("tm", None),
    )
    out_specs = (P("tm", "row", None), P("tm", "row"), P("tm", "row", None))
    return jax.shard_map(
        functools.partial(body, mesh.shape["tm"], mesh.shape["row"]),
        mesh=mesh, in_specs=in_specs, out_specs=out_specs, check_vma=False,
    )
```
